256 devices in a mesh: dp: 8 (over z), tensor: 32 (over x, y, core).
Axes of the slice: x: 4, y: 4, z: 8, core: 2. Of those that a mesh axis runs over, the one named last changes fastest.
Arguments:
- hidden: bfloat16 [256, 16384], P('dp'), may hold values from -6 to 6
- gain: float32 [16384], replicated, may hold values from 0.1 to 1.9
- w_qkv: bfloat16 [16384, 24576], P('dp', 'tensor'), as said below
- cache: bfloat16 [256, 32, 256, 256], P('dp', 'tensor'), as said below
- lengths: int32 [256], P('dp'), may hold values from 32 to 256, as said below
- w_out: bfloat16 [16384, 16384], P('tensor', 'dp'), may hold values from -0.25 to 0.25
Outputs:
- output: bfloat16 [256, 16384], P('dp')
The draws below stay inside these ranges and needn't reach their ends.
Inputs may be any that keep to these rules, and one draw needn't show every extreme that they name: `lengths`: in every draw some row has exactly 256 cached positions. `cache`: head group s holds the keys and values of key-value head s * 8 // 32. `w_qkv`: the key and value columns of head group s are those of key-value head s * 8 // 32.
All inputs are finite; a program needn't handle non-finite values.
Results may differ from the reference program's by a relative error of at most 0.022.
Values may be sent and summed in bfloat16 or wider, within the bound.
A program may use at most 128 MiB of HBM per device.

```python
import jax
import jax.numpy as jnp
from jax import lax

D = 16384
HEADS = 128
KVH = 8
HD = 128
CACHE = 256
BATCH = 256
SLOTS = 32
HPD = 4
SLOTW = 768


def draw_w_qkv(key, part):
    key = jax.random.fold_in(key, 11)
    key_query, key_pair = jax.random.split(key)
    query_part = jax.random.normal(key_query, (D, SLOTS, HPD * HD), jnp.float32)
    pair_part = jax.random.normal(key_pair, (D, KVH, 2 * HD), jnp.float32)
    pair_part = jnp.repeat(pair_part, SLOTS // KVH, axis=1)
    joined = jnp.concatenate([query_part, pair_part], axis=2) * D ** (-0.5)
    return joined.reshape(D, SLOTS * SLOTW).astype(jnp.bfloat16)


def draw_cache(key, part):
    key = jax.random.fold_in(key, 23)
    key_keys, key_values = jax.random.split(key, 2)
    shape = (BATCH, KVH, CACHE, HD)
    keys = jax.random.normal(key_keys, shape, jnp.float32)
    values = jax.random.normal(key_values, shape, jnp.float32)
    joined = jnp.concatenate([keys, values], axis=3)
    return jnp.repeat(joined, SLOTS // KVH, axis=1).astype(jnp.bfloat16)


def draw_lengths(key, part):
    key = jax.random.fold_in(key, 37)
    key_rows, key_pick = jax.random.split(key)
    lower = max(CACHE // 8, 8)
    drawn = jax.random.randint(key_rows, (BATCH,), lower, CACHE + 1)
    chosen = jax.random.randint(key_pick, (), 0, BATCH)
    return jnp.where(jnp.arange(BATCH) == chosen, CACHE, drawn).astype(jnp.int32)


def steps_of(own_key, extent, pieces, low, high):
    level = 1.0
    for dim, shards_of in pieces:
        heights = jax.random.uniform(jax.random.fold_in(jax.random.fold_in(own_key, 6), dim), (shards_of,), jnp.float32, low / len(pieces), high / len(pieces))
        level = level * jnp.repeat(jnp.exp(heights), extent[dim] // shards_of).reshape((-1,) + (1,) * (len(extent) - 1 - dim))
    return level


def scatter_about(key, shape, width, bound, cuts=(), held_as=jnp.bfloat16):
    entries = width * jax.random.normal(key, shape, jnp.float32)
    if cuts:
        entries = entries * steps_of(key, shape, cuts, -0.22, 0.18)
    return jnp.clip(entries, -bound, bound).astype(held_as)


def setup_inputs(seed: int = 0) -> dict:
    arg_keys = jax.random.split(jax.random.key(seed), 7)
    hidden = scatter_about(arg_keys[0], (BATCH, D), 1.0, 6.0, ((0, 8),))
    gain = jnp.clip(1.0 + 0.18 * jax.random.normal(arg_keys[1], (D,), jnp.float32), 0.1, 1.9)
    w_qkv = draw_w_qkv(jax.random.fold_in(arg_keys[6], 71), 0)
    cache = draw_cache(jax.random.fold_in(arg_keys[6], 71), 0)
    lengths = draw_lengths(jax.random.fold_in(arg_keys[6], 71), 0)
    w_out = scatter_about(arg_keys[5], (HEADS * HD, D), (4 * HD) ** -0.5, 0.25, ((0, 32), (1, 8)))
    return dict(hidden=hidden, gain=gain, w_qkv=w_qkv, cache=cache, lengths=lengths, w_out=w_out)


rope_base = 500000.0

def rotate(values, angles):
    half = values.shape[-1] // 2
    first = values[..., :half]
    second = values[..., half:]
    cosine = jnp.cos(angles)
    sine = jnp.sin(angles)
    return jnp.concatenate([first * cosine - second * sine, second * cosine + first * sine], axis=-1)

def reference(hidden, gain, w_qkv, cache, lengths, w_out):
    batch = hidden.shape[0]
    wide = hidden.astype(jnp.float32)
    square_mean = lax.optimization_barrier(jnp.mean(wide * wide, axis=-1, keepdims=True))
    normed = (wide * lax.rsqrt(square_mean + 1e-05) * gain).astype(jnp.bfloat16)
    projected = jnp.dot(normed, w_qkv, preferred_element_type=jnp.float32).reshape(batch, SLOTS, SLOTW)
    queries = projected[..., :HPD * HD].reshape(batch, SLOTS, HPD, HD)
    new_key = projected[..., HPD * HD:HPD * HD + HD]
    new_value = projected[..., HPD * HD + HD:]
    half = HD // 2
    frequency = rope_base ** (-jnp.arange(half, dtype=jnp.float32) * 2.0 / HD)
    angles = lengths.astype(jnp.float32)[:, None] * frequency[None, :]
    queries = rotate(queries, angles[:, None, None, :]).astype(jnp.bfloat16)
    new_key = rotate(new_key, angles[:, None, :]).astype(jnp.bfloat16)
    new_value = new_value.astype(jnp.bfloat16)
    keys = cache[..., :HD].astype(jnp.float32)
    values = cache[..., HD:].astype(jnp.float32)
    scale = 1.0 / HD ** 0.5
    scores = jnp.einsum('bshd,bscd->bshc', queries.astype(jnp.float32), keys) * scale
    own = jnp.einsum('bshd,bsd->bsh', queries.astype(jnp.float32), new_key.astype(jnp.float32)) * scale
    valid = jnp.arange(CACHE)[None, :] < lengths[:, None]
    scores = jnp.where(valid[:, None, None, :], scores, -jnp.inf)
    largest = jnp.maximum(lax.optimization_barrier(jnp.max(scores, axis=-1)), own)
    weights = jnp.exp(scores - largest[..., None])
    own_weight = jnp.exp(own - largest)
    total = lax.optimization_barrier(jnp.sum(weights, axis=-1)) + own_weight
    probs = (weights / total[..., None]).astype(jnp.bfloat16)
    own_prob = (own_weight / total).astype(jnp.bfloat16)
    mixed = jnp.einsum('bshc,bscd->bshd', probs.astype(jnp.float32), values)
    mixed = mixed + own_prob.astype(jnp.float32)[..., None] * new_value.astype(jnp.float32)[:, :, None, :]
    attended = mixed.astype(jnp.bfloat16).reshape(batch, HEADS * HD)
    result = wide + jnp.dot(attended, w_out, preferred_element_type=jnp.float32)
    return result.astype(jnp.bfloat16)
```

```python
import functools
import math

import jax
import jax.numpy as jnp
from jax import lax
from jax.experimental import pallas as pl
from jax.experimental.pallas import tpu as pltpu
from jax.sharding import PartitionSpec as P

DP = 8
CHIPS = 16
ROWS = 16
FEAT = 2048
HD = 128
QW = 512
NEAR = 5
ROPE_BASE = 500000.0
MESH = pl.DeviceIdType.MESH
F32 = jnp.float32
BF16 = jnp.bfloat16
FAR_ORDER = (6, 5, 7, 0, 4, 1, 3)
PLANE_ORDER = (10, 6, 14, 9, 11, 2, 8, 5, 7, 13, 15, 1, 3, 4, 12)


def kernel(
    hid,
    gain,
    wqkv,
    cache,
    lens,
    wout,
    out,
    x_s,
    far_in,
    far_out,
    gain_s,
    wq_s,
    wkv_s,
    wo_s,
    cache_s,
    hrow_s,
    pq_s,
    rq_s,
    pkv_s,
    rkv_s,
    nkv_s,
    at_s,
    acc_s,
    po_s,
    ro_s,
    ps_s,
    r5_s,
    fin_s,
    g_s,
    lsem,
    w_ss,
    w_rs,
    x_ss,
    x_rs,
    xp_ss,
    xp_rs,
    kv_ss,
    kv_rs,
    q_ss,
    q_rs,
    n_ss,
    n_rs,
    a_ss,
    a_rs,
    o_ss,
    o_rs,
    t_ss,
    t_rs,
    f_ss,
    f_rs,
    e_ss,
    e_rs,
    osem,
):
    d = lax.axis_index("dp")
    t = lax.axis_index("tensor")
    k = t % 2
    c = t // 2
    cx = c // 4
    cy = c % 4
    half = c % 2
    row0 = pl.multiple_of(k * ROWS, ROWS)
    sibling = (d, c * 2 + (1 - k))

    def block(g):
        return (d + g + 6) % DP

    def at_block(g):
        return (block(g), t)

    def chip(o):
        px = (cx + o // 4) % 4
        py = (cy + o % 4) % 4
        return px * 4 + py

    def back(o):
        px = (cx + 4 - o // 4) % 4
        py = (cy + 4 - o % 4) % 4
        return px * 4 + py

    def rdma(src, dst, ss, rs, dev):
        return pltpu.make_async_remote_copy(
            src_ref=src, dst_ref=dst, send_sem=ss, recv_sem=rs, device_id=dev, device_id_type=MESH
        )

    def lanes(index):
        return pl.ds(pl.multiple_of(index * 128, 128), 128)

    mine = pl.ds(pl.multiple_of(d * FEAT, FEAT), FEAT)
    l_x = pltpu.make_async_copy(hid.at[pl.ds(row0, ROWS), mine], x_s.at[2], lsem.at[0])
    l_gain = pltpu.make_async_copy(gain.at[:, mine], gain_s, lsem.at[1])
    l_h = pltpu.make_async_copy(hid.at[pl.ds(row0, ROWS), :], hrow_s, lsem.at[2])
    l_wq = pltpu.make_async_copy(wqkv.at[:, pl.ds(0, QW)], wq_s.at[k], lsem.at[3])
    l_wkv = pltpu.make_async_copy(
        wqkv.at[:, pl.ds(pl.multiple_of(QW + half * HD, HD), HD)], wkv_s, lsem.at[4]
    )
    l_cache = pltpu.make_async_copy(cache.at[pl.ds(row0, ROWS), 0], cache_s, lsem.at[5])
    l_wo = pltpu.make_async_copy(wout, wo_s.at[k], lsem.at[6])
    for copy in (l_gain, l_x, l_h, l_wkv, l_wq, l_cache, l_wo):
        copy.start()

    barrier = pltpu.get_barrier_semaphore()
    partners = [at_block(g) for g in FAR_ORDER]
    partners += [(d, chip(o) * 2 + k) for o in PLANE_ORDER]
    partners += [sibling]
    for dev in partners:
        pl.semaphore_signal(barrier, inc=1, device_id=dev, device_id_type=MESH)
    pl.semaphore_wait(barrier, len(partners))

    def x_copy(g):
        to = (d + 2 - g + DP) % DP
        rows = pl.ds(row0, ROWS)
        if g < NEAR:
            return rdma(
                hid.at[rows, pl.ds(pl.multiple_of(to * FEAT, FEAT), FEAT)],
                x_s.at[g],
                x_ss.at[g],
                x_rs.at[g],
                (to, t),
            )
        return rdma(
            hid.at[rows, pl.ds(pl.multiple_of(to * FEAT + c * 128, 128), 128)],
            far_in.at[g - NEAR],
            x_ss.at[g],
            x_rs.at[g],
            (to, t),
        )

    for g in FAR_ORDER:
        x_copy(g).start()
    w_copies = [
        rdma(wqkv.at[:, pl.ds(0, QW)], wq_s.at[k], w_ss.at[0], w_rs.at[0], sibling),
        rdma(wout, wo_s.at[k], w_ss.at[1], w_rs.at[1], sibling),
    ]
    for copy in w_copies:
        copy.start()

    l_h.wait()

    def square(i, total):
        cols = pl.ds(pl.multiple_of(i * 1024, 1024), 1024)
        part = hrow_s[:, cols].astype(F32)
        part = part * part
        for j in range(8):
            total = total + part[:, j * 128 : (j + 1) * 128]
        return total

    squares = lax.fori_loop(0, 16, square, jnp.zeros((ROWS, 128), F32))
    row_scale = lax.rsqrt(jnp.sum(squares, axis=1, keepdims=True) * (1.0 / (DP * FEAT)) + 1e-05)

    row_id = lax.broadcasted_iota(jnp.int32, (ROWS, HD), 0)
    lane_id = lax.broadcasted_iota(jnp.int32, (ROWS, HD), 1)
    length = jnp.zeros((ROWS, HD), jnp.int32)
    for b in range(ROWS):
        length = jnp.where(row_id == b, lens[k * ROWS + b], length)
    pair = jnp.where(lane_id < HD // 2, lane_id, lane_id - HD // 2).astype(F32)
    angle = length.astype(F32) * jnp.exp(pair * (-2.0 * math.log(ROPE_BASE) / HD))
    cosine = jnp.cos(angle)
    sine = jnp.sin(angle)
    sine = jnp.where(lane_id < HD // 2, -sine, sine)

    def rotate(v):
        return v * cosine + pltpu.roll(v, HD // 2, 1) * sine

    l_gain.wait()
    l_x.wait()

    def apply_gain(g):
        x_s[g] = (x_s[g].astype(F32) * gain_s[...]).astype(BF16)

    apply_gain(2)

    for g in (5, 7, 6):
        x_copy(g).wait_recv()
    here = gain_s[:, lanes(c)]
    tiles = (far_in[...].astype(F32) * here.reshape(1, 1, 128)).astype(BF16)
    far_out[...] = tiles
    x_s[pl.ds(NEAR, 3), :, lanes(c)] = tiles

    def xp_copy(o, src):
        return rdma(
            far_out,
            x_s.at[pl.ds(NEAR, 3), :, lanes(src)],
            xp_ss.at[o],
            xp_rs.at[o],
            (d, chip(o) * 2 + k),
        )

    for o in PLANE_ORDER:
        xp_copy(o, c).start()

    for g in (1, 3, 0, 4):
        x_copy(g).wait_recv()
        apply_gain(g)

    def kv_copy(g):
        return rdma(
            pkv_s.at[g], rkv_s.at[(12 - g) % DP], kv_ss.at[g], kv_rs.at[(12 - g) % DP], at_block(g)
        )

    def q_copy(s, g):
        return rdma(
            pq_s.at[s, g],
            rq_s.at[s, (12 - g) % DP],
            q_ss.at[s, g],
            q_rs.at[s, (12 - g) % DP],
            at_block(g),
        )

    def project(lo, n, order):
        lhs = x_s[pl.ds(lo, n)].reshape(n * ROWS, FEAT)
        got = jnp.dot(lhs, wkv_s[...], preferred_element_type=F32)
        pkv_s[pl.ds(lo, n)] = got.astype(BF16).reshape(n, ROWS, HD)
        for g in order:
            kv_copy(g).start()
        for s in range(2):
            for j in range(2):
                got = jnp.dot(
                    lhs, wq_s[s, :, j * 256 : (j + 1) * 256], preferred_element_type=F32
                )
                pq_s[s, pl.ds(lo, n), :, j * 256 : (j + 1) * 256] = got.astype(BF16).reshape(
                    n, ROWS, 256
                )
            for g in order:
                q_copy(s, g).start()

    l_wkv.wait()
    l_wq.wait()
    rdma(
        wqkv.at[:, pl.ds(0, QW)], wq_s.at[1 - k], w_ss.at[0], w_rs.at[0], sibling
    ).wait_recv()
    project(0, NEAR, (0, 4, 1, 3))
    for o in PLANE_ORDER:
        xp_copy(o, back(o)).wait_recv()
    project(NEAR, 3, (6, 5, 7))

    others = (3, 1, 4, 0, 7, 5, 6)
    total = pkv_s[2].astype(F32)
    for g in others:
        kv_copy((12 - g) % DP).wait_recv()
        total = total + rkv_s[g].astype(F32)
    total = total * row_scale
    nkv_s[half] = jnp.where(half == 0, rotate(total), total).astype(BF16)
    beside = cx * 4 + (cy // 2) * 2 + (1 - half)

    def n_copy(which):
        return rdma(
            nkv_s.at[which], nkv_s.at[which], n_ss.at[0], n_rs.at[0], (d, beside * 2 + k)
        )

    n_copy(half).start()

    l_cache.wait()
    wide_row = lax.broadcasted_iota(jnp.int32, (4 * ROWS, HD), 0) % ROWS
    wide_lane = lax.broadcasted_iota(jnp.int32, (256, 4 * ROWS), 1) % ROWS
    position = lax.broadcasted_iota(jnp.int32, (4 * ROWS, 256), 1)
    limit = jnp.concatenate([length[:, :1]] * 4, axis=0)
    scale = 1.0 / HD**0.5

    def a_copy(s, g):
        return rdma(
            at_s.at[s, :, 2],
            at_s.at[s, :, (12 - g) % DP],
            a_ss.at[s, g],
            a_rs.at[s, (12 - g) % DP],
            at_block(g),
        )

    for s in range(2):
        total = pq_s[s, 2].astype(F32)
        for g in others:
            q_copy(s, (12 - g) % DP).wait_recv()
            total = total + rq_s[s, g].astype(F32)
        total = total * row_scale
        queries = jnp.concatenate(
            [rotate(total[:, h * HD : (h + 1) * HD]) for h in range(4)], axis=0
        ).astype(BF16)
        turned = queries.astype(F32).T.astype(BF16)

        def score(i, scores):
            for j in range(4):
                b = i * 4 + j
                got = jnp.dot(cache_s[b, :, :HD], turned, preferred_element_type=F32)
                scores = jnp.where(wide_lane == b, got, scores)
            return scores

        scores = lax.fori_loop(0, 4, score, jnp.zeros((256, 4 * ROWS), F32))
        scores = jnp.where(position < limit, scores.T * scale, -jnp.inf)
        largest = jnp.max(scores, axis=1, keepdims=True)
        weights = jnp.exp(scores - largest)
        weight_sum = jnp.sum(weights, axis=1, keepdims=True)
        weights = weights.astype(BF16)

        def mix(i, mixed):
            for j in range(4):
                b = i * 4 + j
                got = jnp.dot(weights, cache_s[b, :, HD:], preferred_element_type=F32)
                mixed = jnp.where(wide_row == b, got, mixed)
            return mixed

        mixed = lax.fori_loop(0, 4, mix, jnp.zeros((4 * ROWS, HD), F32))
        if s == 0:
            n_copy(1 - half).wait_recv()
        new_key = jnp.concatenate([nkv_s[0].astype(F32)] * 4, axis=0)
        new_value = jnp.concatenate([nkv_s[1].astype(F32)] * 4, axis=0)
        own = jnp.sum(queries.astype(F32) * new_key, axis=1, keepdims=True) * scale
        top = jnp.maximum(largest, own)
        fade = jnp.exp(largest - top)
        own_weight = jnp.exp(own - top)
        attended = (mixed * fade + own_weight * new_value) / (weight_sum * fade + own_weight)
        at_s[s, :, 2] = attended.astype(BF16).reshape(4, ROWS, HD)
        for g in FAR_ORDER:
            a_copy(s, g).start()

    l_wo.wait()
    rdma(wout, wo_s.at[1 - k], w_ss.at[1], w_rs.at[1], sibling).wait_recv()

    def heads(s):
        for g in others:
            a_copy(s, (12 - g) % DP).wait_recv()
        return jnp.concatenate(
            [at_s[s, h].reshape(DP * ROWS, HD) for h in range(4)], axis=1
        )

    lhs0 = heads(0)

    def first(i, carry):
        cols = pl.ds(pl.multiple_of(i * 256, 256), 256)
        acc_s[:, cols] = jnp.dot(lhs0, wo_s[0, :, cols], preferred_element_type=F32)
        return carry

    lax.fori_loop(0, 8, first, 0)
    lhs1 = heads(1)

    def o_copy(to, slot):
        return rdma(po_s.at[to], ro_s.at[slot], o_ss.at[to], o_rs.at[slot], (d, to * 2 + k))

    def second(i, carry):
        p = (c // 2 + 1 + i) % 8
        cols = pl.ds(pl.multiple_of(p * 256, 256), 256)
        got = acc_s[:, cols] + jnp.dot(lhs1, wo_s[1, :, cols], preferred_element_type=F32)
        got = got.astype(BF16)
        for j in range(2):
            to = p * 2 + j
            po_s[to] = got[:, j * 128 : (j + 1) * 128].reshape(DP, ROWS, 128)

            @pl.when(to != c)
            def _():
                o_copy(to, c).start()

        return carry

    lax.fori_loop(0, 8, second, 0)

    total = po_s[c].astype(F32)
    for o in PLANE_ORDER[::-1]:
        src = chip(o)
        o_copy(src, src).wait_recv()
        total = total + ro_s[src].astype(F32)
    ps_s[...] = total.astype(BF16)

    def t_copy(g):
        return rdma(
            ps_s.at[g], r5_s.at[(12 - g) % DP], t_ss.at[g], t_rs.at[(12 - g) % DP], at_block(g)
        )

    for g in FAR_ORDER:
        t_copy(g).start()

    def finish(g, tile):
        cols = pl.ds(pl.multiple_of(block(g) * FEAT + c * 128, 128), 128)
        done = (hrow_s[:, cols].astype(F32) + tile.astype(F32)).astype(BF16)
        fin_s[g] = done
        g_s[g, :, lanes(c)] = done

    finish(2, ps_s[2])
    for g in others:
        t_copy((12 - g) % DP).wait_recv()
        finish(g, r5_s[g])

    def f_copy(o, src):
        return rdma(
            fin_s, g_s.at[:, :, lanes(src)], f_ss.at[o], f_rs.at[o], (d, chip(o) * 2 + k)
        )

    for o in PLANE_ORDER:
        f_copy(o, c).start()
    for o in PLANE_ORDER[::-1]:
        f_copy(o, back(o)).wait_recv()

    def e_copy(g, first_row):
        view = out.at[
            pl.ds(pl.multiple_of(first_row, ROWS), ROWS),
            pl.ds(pl.multiple_of(block(g) * FEAT, FEAT), FEAT),
        ]
        return (
            rdma(g_s.at[g], view, e_ss.at[g], e_rs.at[g], sibling),
            pltpu.make_async_copy(g_s.at[g], view, osem.at[g]),
        )

    for g in range(DP):
        there, local = e_copy(g, row0)
        there.start()
        local.start()

    for g in FAR_ORDER:
        x_copy(g).wait_send()
        kv_copy(g).wait_send()
        t_copy(g).wait_send()
        for s in range(2):
            q_copy(s, g).wait_send()
            a_copy(s, g).wait_send()
    for copy in w_copies:
        copy.wait_send()
    for o in PLANE_ORDER:
        xp_copy(o, c).wait_send()
        f_copy(o, c).wait_send()
        o_copy(chip(o), c).wait_send()
    n_copy(half).wait_send()
    for g in range(DP):
        there, local = e_copy(g, row0)
        there.wait_send()
        local.wait()
        e_copy(g, (1 - k) * ROWS)[0].wait_recv()


def body(hidden, gain, w_qkv, cache, lengths, w_out):
    any_space = pl.BlockSpec(memory_space=pl.ANY)
    vmem = pltpu.VMEM
    dma = pltpu.SemaphoreType.DMA
    scratch = [
        vmem((DP, ROWS, FEAT), BF16),
        vmem((3, ROWS, 128), BF16),
        vmem((3, ROWS, 128), BF16),
        vmem((1, FEAT), F32),
        vmem((2, FEAT, QW), BF16),
        vmem((FEAT, HD), BF16),
        vmem((2, QW, FEAT), BF16),
        vmem((ROWS, 256, 256), BF16),
        vmem((ROWS, DP * FEAT), BF16),
        vmem((2, DP, ROWS, QW), BF16),
        vmem((2, DP, ROWS, QW), BF16),
        vmem((DP, ROWS, HD), BF16),
        vmem((DP, ROWS, HD), BF16),
        vmem((2, ROWS, HD), BF16),
        vmem((2, 4, DP, ROWS, HD), BF16),
        vmem((DP * ROWS, FEAT), F32),
        vmem((CHIPS, DP, ROWS, 128), BF16),
        vmem((CHIPS, DP, ROWS, 128), BF16),
        vmem((DP, ROWS, 128), BF16),
        vmem((DP, ROWS, 128), BF16),
        vmem((DP, ROWS, 128), BF16),
        vmem((DP, ROWS, FEAT), BF16),
        dma((7,)),
        dma((2,)),
        dma((2,)),
        dma((DP,)),
        dma((DP,)),
        dma((CHIPS,)),
        dma((CHIPS,)),
        dma((DP,)),
        dma((DP,)),
        dma((2, DP)),
        dma((2, DP)),
        dma((1,)),
        dma((1,)),
        dma((2, DP)),
        dma((2, DP)),
        dma((CHIPS,)),
        dma((CHIPS,)),
        dma((DP,)),
        dma((DP,)),
        dma((CHIPS,)),
        dma((CHIPS,)),
        dma((DP,)),
        dma((DP,)),
        dma((DP,)),
    ]
    return pl.pallas_call(
        kernel,
        out_shape=jax.ShapeDtypeStruct(hidden.shape, hidden.dtype),
        in_specs=[
            any_space,
            any_space,
            any_space,
            any_space,
            pl.BlockSpec(memory_space=pltpu.SMEM),
            any_space,
        ],
        out_specs=any_space,
        scratch_shapes=scratch,
        compiler_params=pltpu.CompilerParams(
            collective_id=0, has_side_effects=True, vmem_limit_bytes=40 * 1024 * 1024
        ),
    )(hidden, gain.reshape(1, -1), w_qkv, cache, lengths, w_out)


def solution(mesh):
    return jax.shard_map(
        body,
        mesh=mesh,
        in_specs=(
            P("dp", None),
            P(),
            P("dp", "tensor"),
            P("dp", "tensor", None, None),
            P("dp"),
            P("tensor", "dp"),
        ),
        out_specs=P("dp", None),
        check_vma=False,
    )
```

```python
import functools
import math

import jax
import jax.numpy as jnp
from jax import lax
from jax.experimental import pallas as pl
from jax.experimental.pallas import tpu as pltpu
from jax.sharding import PartitionSpec as P

DP = 8
CHIPS = 16
ROWS = 16
FEAT = 2048
HD = 128
QW = 512
NEAR = 5
ROPE_BASE = 500000.0
MESH = pl.DeviceIdType.MESH
F32 = jnp.float32
BF16 = jnp.bfloat16
REL = (7, 0, 1, 2, 6, 3, 4, 5)
MIRROR = (2, 1, 0, 4, 3, 7, 6, 5)
OWN = 1
FAR_ORDER = (6, 5, 7, 3, 4, 0, 2)
NEAR_ORDER = FAR_ORDER[::-1]
PLANE_ORDER = (10, 6, 14, 9, 11, 2, 8, 5, 7, 13, 15, 1, 3, 4, 12)


def kernel(
    hid,
    gain,
    wqkv,
    cache,
    lens,
    wout,
    out,
    raw_s,
    x_s,
    far_out,
    gain_s,
    wq_s,
    wkv_s,
    wo_s,
    cache_s,
    hrow_s,
    pq_s,
    rq_s,
    pkv_s,
    rkv_s,
    nkv_s,
    at_s,
    acc_s,
    po_s,
    ro_s,
    ps_s,
    fin_s,
    lsem,
    w_ss,
    w_rs,
    x_ss,
    x_rs,
    xp_ss,
    xp_rs,
    kv_ss,
    kv_rs,
    q_ss,
    q_rs,
    n_ss,
    n_rs,
    a_ss,
    a_rs,
    o_ss,
    o_rs,
    t_ss,
    t_rs,
    f_ss,
    f_rs,
    e_ss,
    e_rs,
):
    d = lax.axis_index("dp")
    t = lax.axis_index("tensor")
    k = t % 2
    c = t // 2
    cx = c // 4
    cy = c % 4
    half = c % 2
    row0 = pl.multiple_of(k * ROWS, ROWS)
    sibling = (d, c * 2 + (1 - k))
    sent = []

    def go(copy):
        copy.start()
        sent.append(copy)

    def block(g):
        return (d + REL[g]) % DP

    def at_block(g):
        return (block(g), t)

    def chip(o):
        px = (cx + o // 4) % 4
        py = (cy + o % 4) % 4
        return px * 4 + py

    def back(o):
        px = (cx + 4 - o // 4) % 4
        py = (cy + 4 - o % 4) % 4
        return px * 4 + py

    def rdma(src, dst, ss, rs, dev):
        return pltpu.make_async_remote_copy(
            src_ref=src, dst_ref=dst, send_sem=ss, recv_sem=rs, device_id=dev, device_id_type=MESH
        )

    def lanes(index):
        return pl.ds(pl.multiple_of(index * 128, 128), 128)

    def features(index):
        return pl.ds(pl.multiple_of(index * FEAT, FEAT), FEAT)

    l_gain = pltpu.make_async_copy(gain.at[:, features(d)], gain_s, lsem.at[1])
    l_x = pltpu.make_async_copy(hid.at[pl.ds(row0, ROWS), features(d)], raw_s.at[OWN], lsem.at[0])
    l_h = pltpu.make_async_copy(hid.at[pl.ds(row0, ROWS), :], hrow_s, lsem.at[2])
    l_wq = pltpu.make_async_copy(wqkv.at[:, pl.ds(0, QW)], wq_s.at[k], lsem.at[3])
    l_wkv = pltpu.make_async_copy(wqkv.at[:, lanes(4 + half)], wkv_s, lsem.at[4])
    l_cache = pltpu.make_async_copy(cache.at[pl.ds(row0, ROWS), 0], cache_s, lsem.at[5])
    l_wo = pltpu.make_async_copy(wout, wo_s.at[k], lsem.at[6])
    for copy in (l_gain, l_x, l_h, l_wkv, l_wq, l_cache, l_wo):
        copy.start()

    barrier = pltpu.get_barrier_semaphore()
    partners = [at_block(g) for g in FAR_ORDER]
    partners += [(d, chip(o) * 2 + k) for o in PLANE_ORDER]
    partners += [sibling]
    for dev in partners:
        pl.semaphore_signal(barrier, inc=1, device_id=dev, device_id_type=MESH)
    pl.semaphore_wait(barrier, len(partners))

    def x_copy(g):
        to = block(MIRROR[g])
        rows = pl.ds(row0, ROWS)
        if g < NEAR:
            return rdma(
                hid.at[rows, features(to)], raw_s.at[g], x_ss.at[g], x_rs.at[g], (to, t)
            )
        return rdma(
            hid.at[rows, lanes(to * (FEAT // 128) + c)],
            raw_s.at[g, :, lanes(c)],
            x_ss.at[g],
            x_rs.at[g],
            (to, t),
        )

    for g in FAR_ORDER:
        go(x_copy(g))
    go(rdma(wqkv.at[:, pl.ds(0, QW)], wq_s.at[k], w_ss.at[0], w_rs.at[0], sibling))
    go(rdma(wout, wo_s.at[k], w_ss.at[1], w_rs.at[1], sibling))

    l_h.wait()

    def square(i, total):
        cols = pl.ds(pl.multiple_of(i * 1024, 1024), 1024)
        part = hrow_s[:, cols].astype(F32)
        part = part * part
        for j in range(8):
            total = total + part[:, j * 128 : (j + 1) * 128]
        return total

    squares = lax.fori_loop(0, 16, square, jnp.zeros((ROWS, 128), F32))
    row_scale = lax.rsqrt(jnp.sum(squares, axis=1, keepdims=True) * (1.0 / (DP * FEAT)) + 1e-05)

    row_id = lax.broadcasted_iota(jnp.int32, (ROWS, HD), 0)
    lane_id = lax.broadcasted_iota(jnp.int32, (ROWS, HD), 1)
    length = jnp.zeros((ROWS, HD), jnp.int32)
    for b in range(ROWS):
        length = jnp.where(row_id == b, lens[k * ROWS + b], length)
    pair = jnp.where(lane_id < HD // 2, lane_id, lane_id - HD // 2).astype(F32)
    angle = length.astype(F32) * jnp.exp(pair * (-2.0 * math.log(ROPE_BASE) / HD))
    cosine = jnp.cos(angle)
    sine = jnp.sin(angle)
    sine = jnp.where(lane_id < HD // 2, -sine, sine)

    def rotate(v):
        return v * cosine + pltpu.roll(v, HD // 2, 1) * sine

    l_gain.wait()
    l_x.wait()

    def apply_gain(g):
        x_s[g] = (raw_s[g].astype(F32) * gain_s[...]).astype(BF16)

    apply_gain(OWN)

    for g in (5, 7, 6):
        x_copy(g).wait_recv()
    far = pl.ds(NEAR, DP - NEAR)
    tiles = raw_s[far, :, lanes(c)].astype(F32) * gain_s[:, lanes(c)].reshape(1, 1, 128)
    far_out[...] = tiles.astype(BF16)
    x_s[far, :, lanes(c)] = tiles.astype(BF16)

    def xp_copy(o, src):
        return rdma(
            far_out, x_s.at[far, :, lanes(src)], xp_ss.at[o], xp_rs.at[o], (d, chip(o) * 2 + k)
        )

    for o in PLANE_ORDER:
        go(xp_copy(o, c))

    for g in (0, 2, 3, 4):
        x_copy(g).wait_recv()
        apply_gain(g)

    def kv_copy(g):
        m = MIRROR[g]
        return rdma(pkv_s.at[g], rkv_s.at[m], kv_ss.at[g], kv_rs.at[m], at_block(g))

    def q_copy(s, g):
        m = MIRROR[g]
        return rdma(pq_s.at[s, g], rq_s.at[s, m], q_ss.at[s, g], q_rs.at[s, m], at_block(g))

    def project(lo, n, order):
        lhs = x_s[pl.ds(lo, n)].reshape(n * ROWS, FEAT)
        got = jnp.dot(lhs, wkv_s[...], preferred_element_type=F32)
        pkv_s[pl.ds(lo, n)] = got.astype(BF16).reshape(n, ROWS, HD)
        for g in order:
            go(kv_copy(g))
        for s in range(2):
            for j in range(2):
                cols = slice(j * 256, (j + 1) * 256)
                got = jnp.dot(lhs, wq_s[s, :, cols], preferred_element_type=F32)
                pq_s[s, pl.ds(lo, n), :, cols] = got.astype(BF16).reshape(n, ROWS, 256)
            for g in order:
                go(q_copy(s, g))

    l_wkv.wait()
    l_wq.wait()
    rdma(
        wqkv.at[:, pl.ds(0, QW)], wq_s.at[1 - k], w_ss.at[0], w_rs.at[0], sibling
    ).wait_recv()

    project(0, NEAR, (3, 4, 0, 2))

    for o in PLANE_ORDER[::-1]:
        xp_copy(o, back(o)).wait_recv()

    project(NEAR, DP - NEAR, (6, 5, 7))

    total = pkv_s[OWN].astype(F32)
    for g in NEAR_ORDER:
        kv_copy(MIRROR[g]).wait_recv()
        total = total + rkv_s[g].astype(F32)
    total = total * row_scale
    nkv_s[half] = jnp.where(half == 0, rotate(total), total).astype(BF16)
    beside = c + 1 - 2 * half

    def n_copy(which):
        return rdma(
            nkv_s.at[which], nkv_s.at[which], n_ss.at[0], n_rs.at[0], (d, beside * 2 + k)
        )

    go(n_copy(half))

    l_cache.wait()
    wide_row = lax.broadcasted_iota(jnp.int32, (4 * ROWS, HD), 0) % ROWS
    wide_lane = lax.broadcasted_iota(jnp.int32, (256, 4 * ROWS), 1) % ROWS
    position = lax.broadcasted_iota(jnp.int32, (4 * ROWS, 256), 1)
    limit = jnp.concatenate([length[:, :1]] * 4, axis=0)
    scale = 1.0 / HD**0.5

    def a_copy(s, g):
        m = MIRROR[g]
        return rdma(
            at_s.at[s, :, OWN], at_s.at[s, :, m], a_ss.at[s, g], a_rs.at[s, m], at_block(g)
        )

    for s in range(2):
        total = pq_s[s, OWN].astype(F32)
        for g in NEAR_ORDER:
            q_copy(s, MIRROR[g]).wait_recv()
            total = total + rq_s[s, g].astype(F32)
        total = total * row_scale

        queries = jnp.concatenate(
            [rotate(total[:, h * HD : (h + 1) * HD]) for h in range(4)], axis=0
        ).astype(BF16)
        turned = queries.astype(F32).T.astype(BF16)

        def score(i, scores):
            for j in range(4):
                b = i * 4 + j
                got = jnp.dot(cache_s[b, :, :HD], turned, preferred_element_type=F32)
                scores = jnp.where(wide_lane == b, got, scores)
            return scores

        scores = lax.fori_loop(0, 4, score, jnp.zeros((256, 4 * ROWS), F32))
        scores = jnp.where(position < limit, scores.T * scale, -jnp.inf)
        largest = jnp.max(scores, axis=1, keepdims=True)
        weights = jnp.exp(scores - largest)
        weight_sum = jnp.sum(weights, axis=1, keepdims=True)
        weights = weights.astype(BF16)

        def mix(i, mixed):
            for j in range(4):
                b = i * 4 + j
                got = jnp.dot(weights, cache_s[b, :, HD:], preferred_element_type=F32)
                mixed = jnp.where(wide_row == b, got, mixed)
            return mixed

        mixed = lax.fori_loop(0, 4, mix, jnp.zeros((4 * ROWS, HD), F32))
        if s == 0:
            n_copy(1 - half).wait_recv()
        new_key = jnp.concatenate([nkv_s[0].astype(F32)] * 4, axis=0)
        new_value = jnp.concatenate([nkv_s[1].astype(F32)] * 4, axis=0)
        own = jnp.sum(queries.astype(F32) * new_key, axis=1, keepdims=True) * scale
        top = jnp.maximum(largest, own)
        fade = jnp.exp(largest - top)
        own_weight = jnp.exp(own - top)
        attended = (mixed * fade + own_weight * new_value) / (weight_sum * fade + own_weight)
        at_s[s, :, OWN] = attended.astype(BF16).reshape(4, ROWS, HD)
        for g in FAR_ORDER:
            go(a_copy(s, g))

    l_wo.wait()
    rdma(wout, wo_s.at[1 - k], w_ss.at[1], w_rs.at[1], sibling).wait_recv()

    def heads(s):
        for g in NEAR_ORDER:
            a_copy(s, MIRROR[g]).wait_recv()
        return jnp.concatenate([at_s[s, h].reshape(DP * ROWS, HD) for h in range(4)], axis=1)

    def o_copy(to, slot):
        return rdma(po_s.at[to], ro_s.at[slot], o_ss.at[to], o_rs.at[slot], (d, to * 2 + k))

    lhs0 = heads(0)

    def first_half(i, carry):
        cols = pl.ds(pl.multiple_of(i * 256, 256), 256)
        acc_s[:, cols] = jnp.dot(lhs0, wo_s[0, :, cols], preferred_element_type=F32)
        return carry

    lax.fori_loop(0, 8, first_half, 0)
    lhs1 = heads(1)

    def second_half(i, carry):
        p = (cx + 2 + i // 2) % 4 * 2 + (cy // 2 + 1 + i) % 2
        cols = pl.ds(pl.multiple_of(p * 256, 256), 256)
        got = acc_s[:, cols] + jnp.dot(lhs1, wo_s[1, :, cols], preferred_element_type=F32)
        got = got.astype(BF16)
        for j in range(2):
            to = p * 2 + j
            po_s[to] = got[:, j * 128 : (j + 1) * 128].reshape(DP, ROWS, 128)

            @pl.when(to != c)
            def _():
                o_copy(to, c).start()

        return carry

    lax.fori_loop(0, 8, second_half, 0)
    for o in PLANE_ORDER:
        sent.append(o_copy(chip(o), c))

    total = po_s[c].astype(F32)
    for o in PLANE_ORDER[::-1]:
        src = back(o)
        o_copy(src, src).wait_recv()
        total = total + ro_s[src].astype(F32)
    ps_s[...] = (raw_s[:, :, lanes(c)].astype(F32) + total).astype(BF16)

    def t_copy(g):
        return rdma(ps_s.at[g], fin_s.at[d], t_ss.at[g], t_rs.at[MIRROR[g]], at_block(g))

    for g in FAR_ORDER:
        go(t_copy(g))
    fin_s[d] = ps_s[OWN]
    for g in NEAR_ORDER:
        rdma(
            ps_s.at[g], fin_s.at[block(g)], t_ss.at[g], t_rs.at[g], at_block(g)
        ).wait_recv()

    def f_copy(o, src):
        return rdma(
            fin_s, out.at[k, :, :, lanes(src)], f_ss.at[o], f_rs.at[o], (d, chip(o) * 2 + k)
        )

    def e_copy(o, src, half_of):
        view = out.at[half_of, :, :, lanes(src)]
        return rdma(view, view, e_ss.at[o], e_rs.at[o], sibling)

    for o in PLANE_ORDER:
        go(f_copy(o, c))
    out[k, :, :, lanes(c)] = fin_s[...]
    go(e_copy(0, c, k))
    for o in PLANE_ORDER[::-1]:
        f_copy(o, back(o)).wait_recv()
        go(e_copy(o, back(o), k))

    e_copy(0, c, 1 - k).wait_recv()
    for o in PLANE_ORDER[::-1]:
        e_copy(o, back(o), 1 - k).wait_recv()

    for copy in sent:
        copy.wait_send()


def body(hidden, gain, w_qkv, cache, lengths, w_out):
    any_space = pl.BlockSpec(memory_space=pl.ANY)
    vmem = pltpu.VMEM
    dma = pltpu.SemaphoreType.DMA
    scratch = [
        vmem((DP, ROWS, FEAT), BF16),
        vmem((DP, ROWS, FEAT), BF16),
        vmem((DP - NEAR, ROWS, 128), BF16),
        vmem((1, FEAT), F32),
        vmem((2, FEAT, QW), BF16),
        vmem((FEAT, HD), BF16),
        vmem((2, QW, FEAT), BF16),
        vmem((ROWS, 256, 256), BF16),
        vmem((ROWS, DP * FEAT), BF16),
        vmem((2, DP, ROWS, QW), BF16),
        vmem((2, DP, ROWS, QW), BF16),
        vmem((DP, ROWS, HD), BF16),
        vmem((DP, ROWS, HD), BF16),
        vmem((2, ROWS, HD), BF16),
        vmem((2, 4, DP, ROWS, HD), BF16),
        vmem((DP * ROWS, FEAT), F32),
        vmem((CHIPS, DP, ROWS, 128), BF16),
        vmem((CHIPS, DP, ROWS, 128), BF16),
        vmem((DP, ROWS, 128), BF16),
        vmem((DP, ROWS, 128), BF16),
        dma((7,)),
        dma((2,)),
        dma((2,)),
        dma((DP,)),
        dma((DP,)),
        dma((CHIPS,)),
        dma((CHIPS,)),
        dma((DP,)),
        dma((DP,)),
        dma((2, DP)),
        dma((2, DP)),
        dma((1,)),
        dma((1,)),
        dma((2, DP)),
        dma((2, DP)),
        dma((CHIPS,)),
        dma((CHIPS,)),
        dma((DP,)),
        dma((DP,)),
        dma((CHIPS,)),
        dma((CHIPS,)),
        dma((CHIPS,)),
        dma((CHIPS,)),
    ]
    halves = pl.pallas_call(
        kernel,
        out_shape=vmem((2, DP, ROWS, FEAT), BF16),
        in_specs=[
            any_space,
            any_space,
            any_space,
            any_space,
            pl.BlockSpec(memory_space=pltpu.SMEM),
            any_space,
        ],
        out_specs=pl.BlockSpec(memory_space=vmem),
        scratch_shapes=scratch,
        compiler_params=pltpu.CompilerParams(
            collective_id=0, has_side_effects=True, vmem_limit_bytes=60 * 1024 * 1024
        ),
    )(hidden, gain.reshape(1, -1), w_qkv, cache, lengths, w_out)
    tiles = halves.reshape(2, DP, 2, 8, FEAT).transpose(0, 2, 3, 1, 4)
    return tiles.reshape(hidden.shape)


def solution(mesh):
    return jax.shard_map(
        body,
        mesh=mesh,
        in_specs=(
            P("dp", None),
            P(),
            P("dp", "tensor"),
            P("dp", "tensor", None, None),
            P("dp"),
            P("tensor", "dp"),
        ),
        out_specs=P("dp", None),
        check_vma=False,
    )
```

```python
import functools
import math

import jax
import jax.numpy as jnp
from jax import lax
from jax.experimental import pallas as pl
from jax.experimental.pallas import tpu as pltpu
from jax.sharding import PartitionSpec as P

DP = 8
CHIPS = 16
ROWS = 16
FEAT = 2048
HD = 128
QW = 512
NEAR = 3
ROPE_BASE = 500000.0
MESH = pl.DeviceIdType.MESH
F32 = jnp.float32
BF16 = jnp.bfloat16
REL = (7, 0, 1, 2, 6, 3, 4, 5)
MIRROR = (2, 1, 0, 4, 3, 7, 6, 5)
OWN = 1
PARTS = ((1, 0, 2, 3, 4), (5, 7, 6))
FAR_ORDER = (6, 5, 7, 3, 4, 0, 2)
NEAR_ORDER = FAR_ORDER[::-1]
PLANE_ORDER = (10, 6, 14, 9, 11, 2, 8, 5, 7, 13, 15, 1, 3, 4, 12)


def kernel(
    hid,
    gain,
    wqkv,
    cache,
    lens,
    wout,
    out,
    raw_s,
    x_s,
    far_out,
    gain_s,
    wq_s,
    wkv_s,
    wo_s,
    cache_s,
    hrow_s,
    pq_s,
    rq_s,
    pkv_s,
    rkv_s,
    nkv_s,
    at_s,
    acc_s,
    po_s,
    ro_s,
    ps_s,
    fin_s,
    lsem,
    w_ss,
    w_rs,
    x_ss,
    x_rs,
    xp_ss,
    xp_rs,
    kv_ss,
    kv_rs,
    q_ss,
    q_rs,
    n_ss,
    n_rs,
    a_ss,
    a_rs,
    o_ss,
    o_rs,
    t_ss,
    t_rs,
    f_ss,
    f_rs,
    e_ss,
    e_rs,
):
    d = lax.axis_index("dp")
    t = lax.axis_index("tensor")
    k = t % 2
    c = t // 2
    cx = c // 4
    cy = c % 4
    half = c % 2
    row0 = pl.multiple_of(k * ROWS, ROWS)
    sibling = (d, c * 2 + (1 - k))
    sent = []

    def go(copy):
        copy.start()
        sent.append(copy)

    def block(g):
        return (d + REL[g]) % DP

    def at_block(g):
        return (block(g), t)

    def chip(o):
        px = (cx + o // 4) % 4
        py = (cy + o % 4) % 4
        return px * 4 + py

    def back(o):
        px = (cx + 4 - o // 4) % 4
        py = (cy + 4 - o % 4) % 4
        return px * 4 + py

    def rdma(src, dst, ss, rs, dev):
        return pltpu.make_async_remote_copy(
            src_ref=src, dst_ref=dst, send_sem=ss, recv_sem=rs, device_id=dev, device_id_type=MESH
        )

    def lanes(index):
        return pl.ds(pl.multiple_of(index * 128, 128), 128)

    def features(index):
        return pl.ds(pl.multiple_of(index * FEAT, FEAT), FEAT)

    l_gain = pltpu.make_async_copy(gain.at[:, features(d)], gain_s, lsem.at[1])
    l_x = pltpu.make_async_copy(hid.at[pl.ds(row0, ROWS), features(d)], raw_s.at[OWN], lsem.at[0])
    l_h = pltpu.make_async_copy(hid.at[pl.ds(row0, ROWS), :], hrow_s, lsem.at[2])
    l_wq = pltpu.make_async_copy(wqkv.at[:, pl.ds(0, QW)], wq_s.at[k], lsem.at[3])
    l_wkv = pltpu.make_async_copy(wqkv.at[:, lanes(4 + half)], wkv_s, lsem.at[4])
    l_cache = pltpu.make_async_copy(cache.at[pl.ds(row0, ROWS), 0], cache_s, lsem.at[5])
    l_wo = pltpu.make_async_copy(wout, wo_s.at[k], lsem.at[6])
    for copy in (l_gain, l_x, l_h, l_wkv, l_wq, l_cache, l_wo):
        copy.start()

    barrier = pltpu.get_barrier_semaphore()
    partners = [at_block(g) for g in FAR_ORDER]
    partners += [(d, chip(o) * 2 + k) for o in PLANE_ORDER]
    partners += [sibling]
    for dev in partners:
        pl.semaphore_signal(barrier, inc=1, device_id=dev, device_id_type=MESH)
    pl.semaphore_wait(barrier, len(partners))

    def x_copy(g):
        to = block(MIRROR[g])
        rows = pl.ds(row0, ROWS)
        if g < NEAR:
            return rdma(
                hid.at[rows, features(to)], raw_s.at[g], x_ss.at[g], x_rs.at[g], (to, t)
            )
        return rdma(
            hid.at[rows, lanes(to * (FEAT // 128) + c)],
            raw_s.at[g, :, lanes(c)],
            x_ss.at[g],
            x_rs.at[g],
            (to, t),
        )

    for g in FAR_ORDER:
        go(x_copy(g))
    go(rdma(wqkv.at[:, pl.ds(0, QW)], wq_s.at[k], w_ss.at[0], w_rs.at[0], sibling))
    go(rdma(wout, wo_s.at[k], w_ss.at[1], w_rs.at[1], sibling))

    l_h.wait()

    def square(i, total):
        cols = pl.ds(pl.multiple_of(i * 1024, 1024), 1024)
        part = hrow_s[:, cols].astype(F32)
        part = part * part
        for j in range(8):
            total = total + part[:, j * 128 : (j + 1) * 128]
        return total

    squares = lax.fori_loop(0, 16, square, jnp.zeros((ROWS, 128), F32))
    row_scale = lax.rsqrt(jnp.sum(squares, axis=1, keepdims=True) * (1.0 / (DP * FEAT)) + 1e-05)

    row_id = lax.broadcasted_iota(jnp.int32, (ROWS, HD), 0)
    lane_id = lax.broadcasted_iota(jnp.int32, (ROWS, HD), 1)
    length = jnp.zeros((ROWS, HD), jnp.int32)
    for b in range(ROWS):
        length = jnp.where(row_id == b, lens[k * ROWS + b], length)
    pair = jnp.where(lane_id < HD // 2, lane_id, lane_id - HD // 2).astype(F32)
    angle = length.astype(F32) * jnp.exp(pair * (-2.0 * math.log(ROPE_BASE) / HD))
    cosine = jnp.cos(angle)
    sine = jnp.sin(angle)
    sine = jnp.where(lane_id < HD // 2, -sine, sine)

    def rotate(v):
        return v * cosine + pltpu.roll(v, HD // 2, 1) * sine

    l_gain.wait()
    l_x.wait()

    def apply_gain(g):
        x_s[g] = (raw_s[g].astype(F32) * gain_s[...]).astype(BF16)

    apply_gain(OWN)

    for g in (3, 4, 5, 7, 6):
        x_copy(g).wait_recv()
    far = pl.ds(NEAR, DP - NEAR)
    tiles = raw_s[far, :, lanes(c)].astype(F32) * gain_s[:, lanes(c)].reshape(1, 1, 128)
    far_out[...] = tiles.astype(BF16)
    x_s[far, :, lanes(c)] = tiles.astype(BF16)

    def xp_copy(o, src):
        return rdma(
            far_out, x_s.at[far, :, lanes(src)], xp_ss.at[o], xp_rs.at[o], (d, chip(o) * 2 + k)
        )

    for o in PLANE_ORDER:
        go(xp_copy(o, c))

    for g in (0, 2):
        x_copy(g).wait_recv()
        apply_gain(g)

    def kv_copy(g):
        m = MIRROR[g]
        return rdma(pkv_s.at[g], rkv_s.at[m], kv_ss.at[g], kv_rs.at[m], at_block(g))

    def q_copy(s, g):
        m = MIRROR[g]
        return rdma(pq_s.at[s, g], rq_s.at[s, m], q_ss.at[s, g], q_rs.at[s, m], at_block(g))

    def project(lo, n, order):
        lhs = x_s[pl.ds(lo, n)].reshape(n * ROWS, FEAT)
        got = jnp.dot(lhs, wkv_s[...], preferred_element_type=F32)
        pkv_s[pl.ds(lo, n)] = got.astype(BF16).reshape(n, ROWS, HD)
        for g in order:
            go(kv_copy(g))
        for s in range(2):
            for j in range(2):
                cols = slice(j * 256, (j + 1) * 256)
                got = jnp.dot(lhs, wq_s[s, :, cols], preferred_element_type=F32)
                pq_s[s, pl.ds(lo, n), :, cols] = got.astype(BF16).reshape(n, ROWS, 256)
            for g in order:
                go(q_copy(s, g))

    l_wkv.wait()
    l_wq.wait()
    rdma(
        wqkv.at[:, pl.ds(0, QW)], wq_s.at[1 - k], w_ss.at[0], w_rs.at[0], sibling
    ).wait_recv()

    project(0, NEAR, (0, 2))

    for o in PLANE_ORDER[::-1]:
        xp_copy(o, back(o)).wait_recv()

    project(NEAR, DP - NEAR, (6, 5, 7, 3, 4))

    total = pkv_s[OWN].astype(F32)
    for g in NEAR_ORDER:
        kv_copy(MIRROR[g]).wait_recv()
        total = total + rkv_s[g].astype(F32)
    total = total * row_scale
    nkv_s[half] = jnp.where(half == 0, rotate(total), total).astype(BF16)
    beside = c + 1 - 2 * half

    def n_copy(which):
        return rdma(
            nkv_s.at[which], nkv_s.at[which], n_ss.at[0], n_rs.at[0], (d, beside * 2 + k)
        )

    go(n_copy(half))

    l_cache.wait()
    wide_row = lax.broadcasted_iota(jnp.int32, (4 * ROWS, HD), 0) % ROWS
    wide_lane = lax.broadcasted_iota(jnp.int32, (256, 4 * ROWS), 1) % ROWS
    position = lax.broadcasted_iota(jnp.int32, (4 * ROWS, 256), 1)
    limit = jnp.concatenate([length[:, :1]] * 4, axis=0)
    scale = 1.0 / HD**0.5

    def a_copy(s, g):
        m = MIRROR[g]
        return rdma(
            at_s.at[s, :, OWN], at_s.at[s, :, m], a_ss.at[s, g], a_rs.at[s, m], at_block(g)
        )

    for s in range(2):
        total = pq_s[s, OWN].astype(F32)
        for g in NEAR_ORDER:
            q_copy(s, MIRROR[g]).wait_recv()
            total = total + rq_s[s, g].astype(F32)
        total = total * row_scale

        queries = jnp.concatenate(
            [rotate(total[:, h * HD : (h + 1) * HD]) for h in range(4)], axis=0
        ).astype(BF16)
        turned = queries.astype(F32).T.astype(BF16)

        def score(i, scores):
            for j in range(4):
                b = i * 4 + j
                got = jnp.dot(cache_s[b, :, :HD], turned, preferred_element_type=F32)
                scores = jnp.where(wide_lane == b, got, scores)
            return scores

        scores = lax.fori_loop(0, 4, score, jnp.zeros((256, 4 * ROWS), F32))
        scores = jnp.where(position < limit, scores.T * scale, -jnp.inf)
        largest = jnp.max(scores, axis=1, keepdims=True)
        weights = jnp.exp(scores - largest)
        weight_sum = jnp.sum(weights, axis=1, keepdims=True)
        weights = weights.astype(BF16)

        def mix(i, mixed):
            for j in range(4):
                b = i * 4 + j
                got = jnp.dot(weights, cache_s[b, :, HD:], preferred_element_type=F32)
                mixed = jnp.where(wide_row == b, got, mixed)
            return mixed

        mixed = lax.fori_loop(0, 4, mix, jnp.zeros((4 * ROWS, HD), F32))
        if s == 0:
            n_copy(1 - half).wait_recv()
        new_key = jnp.concatenate([nkv_s[0].astype(F32)] * 4, axis=0)
        new_value = jnp.concatenate([nkv_s[1].astype(F32)] * 4, axis=0)
        own = jnp.sum(queries.astype(F32) * new_key, axis=1, keepdims=True) * scale
        top = jnp.maximum(largest, own)
        fade = jnp.exp(largest - top)
        own_weight = jnp.exp(own - top)
        attended = (mixed * fade + own_weight * new_value) / (weight_sum * fade + own_weight)
        at_s[s, :, OWN] = attended.astype(BF16).reshape(4, ROWS, HD)
        for g in FAR_ORDER:
            go(a_copy(s, g))

    l_wo.wait()
    rdma(wout, wo_s.at[1 - k], w_ss.at[1], w_rs.at[1], sibling).wait_recv()

    def heads(s):
        for g in NEAR_ORDER:
            a_copy(s, MIRROR[g]).wait_recv()
        return jnp.concatenate([at_s[s, h].reshape(DP * ROWS, HD) for h in range(4)], axis=1)

    def o_copy(to, slot):
        return rdma(po_s.at[to], ro_s.at[slot], o_ss.at[to], o_rs.at[slot], (d, to * 2 + k))

    lhs0 = heads(0)

    def first_half(i, carry):
        cols = pl.ds(pl.multiple_of(i * 256, 256), 256)
        acc_s[:, cols] = jnp.dot(lhs0, wo_s[0, :, cols], preferred_element_type=F32)
        return carry

    lax.fori_loop(0, 8, first_half, 0)
    lhs1 = heads(1)

    def second_half(i, carry):
        p = (cx + 2 + i // 2) % 4 * 2 + (cy // 2 + 1 + i) % 2
        cols = pl.ds(pl.multiple_of(p * 256, 256), 256)
        got = acc_s[:, cols] + jnp.dot(lhs1, wo_s[1, :, cols], preferred_element_type=F32)
        got = got.astype(BF16)
        for j in range(2):
            to = p * 2 + j
            po_s[to] = got[:, j * 128 : (j + 1) * 128].reshape(DP, ROWS, 128)

            @pl.when(to != c)
            def _():
                o_copy(to, c).start()

        return carry

    lax.fori_loop(0, 8, second_half, 0)
    for o in PLANE_ORDER:
        sent.append(o_copy(chip(o), c))

    total = po_s[c].astype(F32)
    for o in PLANE_ORDER[::-1]:
        src = back(o)
        o_copy(src, src).wait_recv()
        total = total + ro_s[src].astype(F32)
    ps_s[...] = (raw_s[:, :, lanes(c)].astype(F32) + total).astype(BF16)

    def t_copy(g):
        return rdma(ps_s.at[g], fin_s.at[d], t_ss.at[g], t_rs.at[MIRROR[g]], at_block(g))

    for g in FAR_ORDER:
        go(t_copy(g))
    fin_s[d] = ps_s[OWN]

    def f_copy(q, o, src, which):
        return rdma(
            fin_s.at[which],
            out.at[k, which, :, lanes(src)],
            f_ss.at[q, o],
            f_rs.at[q, o],
            (d, chip(o) * 2 + k),
        )

    def f_all(q, o, src):
        return f_copy(q, o, src, pl.ds(0, len(PARTS[q])))

    for q, part in enumerate(PARTS):
        for g in part:
            if g != OWN:
                rdma(
                    ps_s.at[g], fin_s.at[block(g)], t_ss.at[g], t_rs.at[g], at_block(g)
                ).wait_recv()
        for o in PLANE_ORDER:
            for g in part:
                f_copy(q, o, c, block(g)).start()
            sent.append(f_all(q, o, c))

    def e_copy(o, src, half_of):
        view = out.at[half_of, :, :, lanes(src)]
        return rdma(view, view, e_ss.at[o], e_rs.at[o], sibling)

    out[k, :, :, lanes(c)] = fin_s[...]
    go(e_copy(0, c, k))
    for o in PLANE_ORDER[::-1]:
        for q in range(len(PARTS)):
            f_all(q, o, back(o)).wait_recv()
        go(e_copy(o, back(o), k))

    e_copy(0, c, 1 - k).wait_recv()
    for o in PLANE_ORDER[::-1]:
        e_copy(o, back(o), 1 - k).wait_recv()

    for copy in sent:
        copy.wait_send()


def body(hidden, gain, w_qkv, cache, lengths, w_out):
    any_space = pl.BlockSpec(memory_space=pl.ANY)
    vmem = pltpu.VMEM
    dma = pltpu.SemaphoreType.DMA
    scratch = [
        vmem((DP, ROWS, FEAT), BF16),
        vmem((DP, ROWS, FEAT), BF16),
        vmem((DP - NEAR, ROWS, 128), BF16),
        vmem((1, FEAT), F32),
        vmem((2, FEAT, QW), BF16),
        vmem((FEAT, HD), BF16),
        vmem((2, QW, FEAT), BF16),
        vmem((ROWS, 256, 256), BF16),
        vmem((ROWS, DP * FEAT), BF16),
        vmem((2, DP, ROWS, QW), BF16),
        vmem((2, DP, ROWS, QW), BF16),
        vmem((DP, ROWS, HD), BF16),
        vmem((DP, ROWS, HD), BF16),
        vmem((2, ROWS, HD), BF16),
        vmem((2, 4, DP, ROWS, HD), BF16),
        vmem((DP * ROWS, FEAT), F32),
        vmem((CHIPS, DP, ROWS, 128), BF16),
        vmem((CHIPS, DP, ROWS, 128), BF16),
        vmem((DP, ROWS, 128), BF16),
        vmem((DP, ROWS, 128), BF16),
        dma((7,)),
        dma((2,)),
        dma((2,)),
        dma((DP,)),
        dma((DP,)),
        dma((CHIPS,)),
        dma((CHIPS,)),
        dma((DP,)),
        dma((DP,)),
        dma((2, DP)),
        dma((2, DP)),
        dma((1,)),
        dma((1,)),
        dma((2, DP)),
        dma((2, DP)),
        dma((CHIPS,)),
        dma((CHIPS,)),
        dma((DP,)),
        dma((DP,)),
        dma((len(PARTS), CHIPS)),
        dma((len(PARTS), CHIPS)),
        dma((CHIPS,)),
        dma((CHIPS,)),
    ]
    halves = pl.pallas_call(
        kernel,
        out_shape=vmem((2, DP, ROWS, FEAT), BF16),
        in_specs=[
            any_space,
            any_space,
            any_space,
            any_space,
            pl.BlockSpec(memory_space=pltpu.SMEM),
            any_space,
        ],
        out_specs=pl.BlockSpec(memory_space=vmem),
        scratch_shapes=scratch,
        compiler_params=pltpu.CompilerParams(
            collective_id=0, has_side_effects=True, vmem_limit_bytes=60 * 1024 * 1024
        ),
    )(hidden, gain.reshape(1, -1), w_qkv, cache, lengths, w_out)
    tiles = halves.reshape(2, DP, 2, 8, FEAT).transpose(0, 2, 3, 1, 4)
    return tiles.reshape(hidden.shape)


def solution(mesh):
    return jax.shard_map(
        body,
        mesh=mesh,
        in_specs=(
            P("dp", None),
            P(),
            P("dp", "tensor"),
            P("dp", "tensor", None, None),
            P("dp"),
            P("tensor", "dp"),
        ),
        out_specs=P("dp", None),
        check_vma=False,
    )
```

```python
import functools
import math

import jax
import jax.numpy as jnp
from jax import lax
from jax.experimental import pallas as pl
from jax.experimental.pallas import tpu as pltpu
from jax.sharding import PartitionSpec as P

DP = 8
CHIPS = 16
ROWS = 16
FEAT = 2048
HD = 128
QW = 512
NEAR = 3
ROPE_BASE = 500000.0
MESH = pl.DeviceIdType.MESH
F32 = jnp.float32
BF16 = jnp.bfloat16
REL = (7, 0, 1, 2, 6, 3, 4, 5)
MIRROR = (2, 1, 0, 4, 3, 7, 6, 5)
OWN = 1
PARTS = ((1, 0, 2), (3, 4, 5, 7, 6))
FAR_ORDER = (6, 5, 7, 3, 4, 0, 2)
NEAR_ORDER = FAR_ORDER[::-1]
PLANE_ORDER = (10, 6, 14, 9, 11, 2, 8, 5, 7, 13, 15, 1, 3, 4, 12)


def kernel(
    hid,
    gain,
    wqkv,
    cache,
    lens,
    wout,
    out,
    raw_s,
    x_s,
    far_out,
    gain_s,
    wq_s,
    wkv_s,
    wo_s,
    cache_s,
    hrow_s,
    pq_s,
    rq_s,
    pkv_s,
    rkv_s,
    nkv_s,
    at_s,
    acc_s,
    po_s,
    ro_s,
    ps_s,
    fin_s,
    lsem,
    w_ss,
    w_rs,
    x_ss,
    x_rs,
    xp_ss,
    xp_rs,
    kv_ss,
    kv_rs,
    q_ss,
    q_rs,
    n_ss,
    n_rs,
    a_ss,
    a_rs,
    o_ss,
    o_rs,
    t_ss,
    t_rs,
    f_ss,
    f_rs,
    e_ss,
    e_rs,
):
    d = lax.axis_index("dp")
    t = lax.axis_index("tensor")
    k = t % 2
    c = t // 2
    cx = c // 4
    cy = c % 4
    half = c % 2
    row0 = pl.multiple_of(k * ROWS, ROWS)
    sibling = (d, c * 2 + (1 - k))
    sent = []

    def go(copy):
        copy.start()
        sent.append(copy)

    def block(g):
        return (d + REL[g]) % DP

    def at_block(g):
        return (block(g), t)

    def chip(o):
        px = (cx + o // 4) % 4
        py = (cy + o % 4) % 4
        return px * 4 + py

    def back(o):
        px = (cx + 4 - o // 4) % 4
        py = (cy + 4 - o % 4) % 4
        return px * 4 + py

    def rdma(src, dst, ss, rs, dev):
        return pltpu.make_async_remote_copy(
            src_ref=src, dst_ref=dst, send_sem=ss, recv_sem=rs, device_id=dev, device_id_type=MESH
        )

    def lanes(index):
        return pl.ds(pl.multiple_of(index * 128, 128), 128)

    def features(index):
        return pl.ds(pl.multiple_of(index * FEAT, FEAT), FEAT)

    l_gain = pltpu.make_async_copy(gain.at[:, features(d)], gain_s, lsem.at[1])
    l_x = pltpu.make_async_copy(hid.at[pl.ds(row0, ROWS), features(d)], raw_s.at[OWN], lsem.at[0])
    l_h = pltpu.make_async_copy(hid.at[pl.ds(row0, ROWS), :], hrow_s, lsem.at[2])
    l_wq = pltpu.make_async_copy(wqkv.at[:, pl.ds(0, QW)], wq_s.at[k], lsem.at[3])
    l_wkv = pltpu.make_async_copy(wqkv.at[:, lanes(4 + half)], wkv_s, lsem.at[4])
    l_cache = pltpu.make_async_copy(cache.at[pl.ds(row0, ROWS), 0], cache_s, lsem.at[5])
    l_wo = pltpu.make_async_copy(wout, wo_s.at[k], lsem.at[6])
    for copy in (l_gain, l_x, l_h, l_wkv, l_wq, l_cache, l_wo):
        copy.start()

    barrier = pltpu.get_barrier_semaphore()
    partners = [at_block(g) for g in FAR_ORDER]
    partners += [(d, chip(o) * 2 + k) for o in PLANE_ORDER]
    partners += [sibling]
    for dev in partners:
        pl.semaphore_signal(barrier, inc=1, device_id=dev, device_id_type=MESH)
    pl.semaphore_wait(barrier, len(partners))

    def x_copy(g):
        to = block(MIRROR[g])
        rows = pl.ds(row0, ROWS)
        if g < NEAR:
            return rdma(
                hid.at[rows, features(to)], raw_s.at[g], x_ss.at[g], x_rs.at[g], (to, t)
            )
        return rdma(
            hid.at[rows, lanes(to * (FEAT // 128) + c)],
            raw_s.at[g, :, lanes(c)],
            x_ss.at[g],
            x_rs.at[g],
            (to, t),
        )

    for g in FAR_ORDER:
        go(x_copy(g))
    go(rdma(wqkv.at[:, pl.ds(0, QW)], wq_s.at[k], w_ss.at[0], w_rs.at[0], sibling))
    go(rdma(wout, wo_s.at[k], w_ss.at[1], w_rs.at[1], sibling))

    l_h.wait()

    def square(i, total):
        cols = pl.ds(pl.multiple_of(i * 1024, 1024), 1024)
        part = hrow_s[:, cols].astype(F32)
        part = part * part
        for j in range(8):
            total = total + part[:, j * 128 : (j + 1) * 128]
        return total

    squares = lax.fori_loop(0, 16, square, jnp.zeros((ROWS, 128), F32))
    row_scale = lax.rsqrt(jnp.sum(squares, axis=1, keepdims=True) * (1.0 / (DP * FEAT)) + 1e-05)

    row_id = lax.broadcasted_iota(jnp.int32, (ROWS, HD), 0)
    lane_id = lax.broadcasted_iota(jnp.int32, (ROWS, HD), 1)
    length = jnp.zeros((ROWS, HD), jnp.int32)
    for b in range(ROWS):
        length = jnp.where(row_id == b, lens[k * ROWS + b], length)
    pair = jnp.where(lane_id < HD // 2, lane_id, lane_id - HD // 2).astype(F32)
    angle = length.astype(F32) * jnp.exp(pair * (-2.0 * math.log(ROPE_BASE) / HD))
    cosine = jnp.cos(angle)
    sine = jnp.sin(angle)
    sine = jnp.where(lane_id < HD // 2, -sine, sine)

    def rotate(v):
        return v * cosine + pltpu.roll(v, HD // 2, 1) * sine

    l_gain.wait()
    l_x.wait()

    def apply_gain(g):
        x_s[g] = (raw_s[g].astype(F32) * gain_s[...]).astype(BF16)

    apply_gain(OWN)

    for g in (3, 4, 5, 7, 6):
        x_copy(g).wait_recv()
    far = pl.ds(NEAR, DP - NEAR)
    tiles = raw_s[far, :, lanes(c)].astype(F32) * gain_s[:, lanes(c)].reshape(1, 1, 128)
    far_out[...] = tiles.astype(BF16)
    x_s[far, :, lanes(c)] = tiles.astype(BF16)

    def xp_copy(o, src):
        return rdma(
            far_out, x_s.at[far, :, lanes(src)], xp_ss.at[o], xp_rs.at[o], (d, chip(o) * 2 + k)
        )

    for o in PLANE_ORDER:
        go(xp_copy(o, c))

    for g in (0, 2):
        x_copy(g).wait_recv()
        apply_gain(g)

    def kv_copy(g):
        m = MIRROR[g]
        return rdma(pkv_s.at[g], rkv_s.at[m], kv_ss.at[g], kv_rs.at[m], at_block(g))

    def q_copy(s, g):
        m = MIRROR[g]
        return rdma(pq_s.at[s, g], rq_s.at[s, m], q_ss.at[s, g], q_rs.at[s, m], at_block(g))

    def project(lo, n, order):
        lhs = x_s[pl.ds(lo, n)].reshape(n * ROWS, FEAT)
        got = jnp.dot(lhs, wkv_s[...], preferred_element_type=F32)
        pkv_s[pl.ds(lo, n)] = got.astype(BF16).reshape(n, ROWS, HD)
        for g in order:
            go(kv_copy(g))
        for s in range(2):
            for j in range(2):
                cols = slice(j * 256, (j + 1) * 256)
                got = jnp.dot(lhs, wq_s[s, :, cols], preferred_element_type=F32)
                pq_s[s, pl.ds(lo, n), :, cols] = got.astype(BF16).reshape(n, ROWS, 256)
            for g in order:
                go(q_copy(s, g))

    l_wkv.wait()
    l_wq.wait()
    rdma(
        wqkv.at[:, pl.ds(0, QW)], wq_s.at[1 - k], w_ss.at[0], w_rs.at[0], sibling
    ).wait_recv()

    project(0, NEAR, (0, 2))

    for o in PLANE_ORDER[::-1]:
        xp_copy(o, back(o)).wait_recv()

    project(NEAR, DP - NEAR, (6, 5, 7, 3, 4))

    total = pkv_s[OWN].astype(F32)
    for g in NEAR_ORDER:
        kv_copy(MIRROR[g]).wait_recv()
        total = total + rkv_s[g].astype(F32)
    total = total * row_scale
    nkv_s[half] = jnp.where(half == 0, rotate(total), total).astype(BF16)
    beside = c + 1 - 2 * half

    def n_copy(which):
        return rdma(
            nkv_s.at[which], nkv_s.at[which], n_ss.at[0], n_rs.at[0], (d, beside * 2 + k)
        )

    go(n_copy(half))

    l_cache.wait()
    wide_row = lax.broadcasted_iota(jnp.int32, (4 * ROWS, HD), 0) % ROWS
    wide_lane = lax.broadcasted_iota(jnp.int32, (256, 4 * ROWS), 1) % ROWS
    position = lax.broadcasted_iota(jnp.int32, (4 * ROWS, 256), 1)
    limit = jnp.concatenate([length[:, :1]] * 4, axis=0)
    scale = 1.0 / HD**0.5

    def a_copy(s, g):
        m = MIRROR[g]
        return rdma(
            at_s.at[s, :, OWN], at_s.at[s, :, m], a_ss.at[s, g], a_rs.at[s, m], at_block(g)
        )

    for s in range(2):
        total = pq_s[s, OWN].astype(F32)
        for g in NEAR_ORDER:
            q_copy(s, MIRROR[g]).wait_recv()
            total = total + rq_s[s, g].astype(F32)
        total = total * row_scale

        queries = jnp.concatenate(
            [rotate(total[:, h * HD : (h + 1) * HD]) for h in range(4)], axis=0
        ).astype(BF16)
        turned = queries.astype(F32).T.astype(BF16)

        def score(i, scores):
            for j in range(4):
                b = i * 4 + j
                got = jnp.dot(cache_s[b, :, :HD], turned, preferred_element_type=F32)
                scores = jnp.where(wide_lane == b, got, scores)
            return scores

        scores = lax.fori_loop(0, 4, score, jnp.zeros((256, 4 * ROWS), F32))
        scores = jnp.where(position < limit, scores.T * scale, -jnp.inf)
        largest = jnp.max(scores, axis=1, keepdims=True)
        weights = jnp.exp(scores - largest)
        weight_sum = jnp.sum(weights, axis=1, keepdims=True)
        weights = weights.astype(BF16)

        def mix(i, mixed):
            for j in range(4):
                b = i * 4 + j
                got = jnp.dot(weights, cache_s[b, :, HD:], preferred_element_type=F32)
                mixed = jnp.where(wide_row == b, got, mixed)
            return mixed

        mixed = lax.fori_loop(0, 4, mix, jnp.zeros((4 * ROWS, HD), F32))
        if s == 0:
            n_copy(1 - half).wait_recv()
        new_key = jnp.concatenate([nkv_s[0].astype(F32)] * 4, axis=0)
        new_value = jnp.concatenate([nkv_s[1].astype(F32)] * 4, axis=0)
        own = jnp.sum(queries.astype(F32) * new_key, axis=1, keepdims=True) * scale
        top = jnp.maximum(largest, own)
        fade = jnp.exp(largest - top)
        own_weight = jnp.exp(own - top)
        attended = (mixed * fade + own_weight * new_value) / (weight_sum * fade + own_weight)
        at_s[s, :, OWN] = attended.astype(BF16).reshape(4, ROWS, HD)
        for g in FAR_ORDER:
            go(a_copy(s, g))

    l_wo.wait()
    rdma(wout, wo_s.at[1 - k], w_ss.at[1], w_rs.at[1], sibling).wait_recv()

    def heads(s):
        for g in NEAR_ORDER:
            a_copy(s, MIRROR[g]).wait_recv()
        return jnp.concatenate([at_s[s, h].reshape(DP * ROWS, HD) for h in range(4)], axis=1)

    def o_copy(to, slot):
        return rdma(po_s.at[to], ro_s.at[slot], o_ss.at[to], o_rs.at[slot], (d, to * 2 + k))

    lhs0 = heads(0)

    def first_half(i, carry):
        cols = pl.ds(pl.multiple_of(i * 256, 256), 256)
        acc_s[:, cols] = jnp.dot(lhs0, wo_s[0, :, cols], preferred_element_type=F32)
        return carry

    lax.fori_loop(0, 8, first_half, 0)
    lhs1 = heads(1)

    def second_half(i, carry):
        p = (cx + 2 + i // 2) % 4 * 2 + (cy // 2 + 1 + i) % 2
        cols = pl.ds(pl.multiple_of(p * 256, 256), 256)
        got = acc_s[:, cols] + jnp.dot(lhs1, wo_s[1, :, cols], preferred_element_type=F32)
        got = got.astype(BF16)
        for j in range(2):
            to = p * 2 + j
            po_s[to] = got[:, j * 128 : (j + 1) * 128].reshape(DP, ROWS, 128)

            @pl.when(to != c)
            def _():
                o_copy(to, c).start()

        return carry

    lax.fori_loop(0, 8, second_half, 0)
    for o in PLANE_ORDER:
        sent.append(o_copy(chip(o), c))

    total = po_s[c].astype(F32)
    for o in PLANE_ORDER[::-1]:
        src = back(o)
        o_copy(src, src).wait_recv()
        total = total + ro_s[src].astype(F32)
    ps_s[...] = (raw_s[:, :, lanes(c)].astype(F32) + total).astype(BF16)

    def t_copy(g):
        return rdma(ps_s.at[g], fin_s.at[d], t_ss.at[g], t_rs.at[MIRROR[g]], at_block(g))

    for g in FAR_ORDER:
        go(t_copy(g))
    fin_s[d] = ps_s[OWN]

    def f_copy(q, o, src, which):
        return rdma(
            fin_s.at[which],
            out.at[k, which, :, lanes(src)],
            f_ss.at[q, o],
            f_rs.at[q, o],
            (d, chip(o) * 2 + k),
        )

    def f_all(q, o, src):
        return f_copy(q, o, src, pl.ds(0, len(PARTS[q])))

    for q, part in enumerate(PARTS):
        for g in part:
            if g != OWN:
                rdma(
                    ps_s.at[g], fin_s.at[block(g)], t_ss.at[g], t_rs.at[g], at_block(g)
                ).wait_recv()
        for o in PLANE_ORDER:
            for g in part:
                f_copy(q, o, c, block(g)).start()
            sent.append(f_all(q, o, c))

    def e_copy(o, src, half_of):
        view = out.at[half_of, :, :, lanes(src)]
        return rdma(view, view, e_ss.at[o], e_rs.at[o], sibling)

    out[k, :, :, lanes(c)] = fin_s[...]
    go(e_copy(0, c, k))
    for o in PLANE_ORDER[::-1]:
        for q in range(len(PARTS)):
            f_all(q, o, back(o)).wait_recv()
        go(e_copy(o, back(o), k))

    e_copy(0, c, 1 - k).wait_recv()
    for o in PLANE_ORDER[::-1]:
        e_copy(o, back(o), 1 - k).wait_recv()

    for copy in sent:
        copy.wait_send()


def body(hidden, gain, w_qkv, cache, lengths, w_out):
    any_space = pl.BlockSpec(memory_space=pl.ANY)
    vmem = pltpu.VMEM
    dma = pltpu.SemaphoreType.DMA
    scratch = [
        vmem((DP, ROWS, FEAT), BF16),
        vmem((DP, ROWS, FEAT), BF16),
        vmem((DP - NEAR, ROWS, 128), BF16),
        vmem((1, FEAT), F32),
        vmem((2, FEAT, QW), BF16),
        vmem((FEAT, HD), BF16),
        vmem((2, QW, FEAT), BF16),
        vmem((ROWS, 256, 256), BF16),
        vmem((ROWS, DP * FEAT), BF16),
        vmem((2, DP, ROWS, QW), BF16),
        vmem((2, DP, ROWS, QW), BF16),
        vmem((DP, ROWS, HD), BF16),
        vmem((DP, ROWS, HD), BF16),
        vmem((2, ROWS, HD), BF16),
        vmem((2, 4, DP, ROWS, HD), BF16),
        vmem((DP * ROWS, FEAT), F32),
        vmem((CHIPS, DP, ROWS, 128), BF16),
        vmem((CHIPS, DP, ROWS, 128), BF16),
        vmem((DP, ROWS, 128), BF16),
        vmem((DP, ROWS, 128), BF16),
        dma((7,)),
        dma((2,)),
        dma((2,)),
        dma((DP,)),
        dma((DP,)),
        dma((CHIPS,)),
        dma((CHIPS,)),
        dma((DP,)),
        dma((DP,)),
        dma((2, DP)),
        dma((2, DP)),
        dma((1,)),
        dma((1,)),
        dma((2, DP)),
        dma((2, DP)),
        dma((CHIPS,)),
        dma((CHIPS,)),
        dma((DP,)),
        dma((DP,)),
        dma((len(PARTS), CHIPS)),
        dma((len(PARTS), CHIPS)),
        dma((CHIPS,)),
        dma((CHIPS,)),
    ]
    halves = pl.pallas_call(
        kernel,
        out_shape=vmem((2, DP, ROWS, FEAT), BF16),
        in_specs=[
            any_space,
            any_space,
            any_space,
            any_space,
            pl.BlockSpec(memory_space=pltpu.SMEM),
            any_space,
        ],
        out_specs=pl.BlockSpec(memory_space=vmem),
        scratch_shapes=scratch,
        compiler_params=pltpu.CompilerParams(
            collective_id=0, has_side_effects=True, vmem_limit_bytes=60 * 1024 * 1024
        ),
    )(hidden, gain.reshape(1, -1), w_qkv, cache, lengths, w_out)
    tiles = halves.reshape(2, DP, 2, 8, FEAT).transpose(0, 2, 3, 1, 4)
    return tiles.reshape(hidden.shape)


def solution(mesh):
    return jax.shard_map(
        body,
        mesh=mesh,
        in_specs=(
            P("dp", None),
            P(),
            P("dp", "tensor"),
            P("dp", "tensor", None, None),
            P("dp"),
            P("tensor", "dp"),
        ),
        out_specs=P("dp", None),
        check_vma=False,
    )
```

```python
import functools
import math

import jax
import jax.numpy as jnp
from jax import lax
from jax.experimental import pallas as pl
from jax.experimental.pallas import tpu as pltpu
from jax.sharding import PartitionSpec as P

DP = 8
CHIPS = 16
ROWS = 16
FEAT = 2048
HD = 128
QW = 512
NEAR = 3
ROPE_BASE = 500000.0
MESH = pl.DeviceIdType.MESH
F32 = jnp.float32
BF16 = jnp.bfloat16
REL = (7, 0, 1, 2, 6, 3, 4, 5)
MIRROR = (2, 1, 0, 4, 3, 7, 6, 5)
OWN = 1
PARTS = ((1, 0, 2), (3, 4, 5, 7, 6))
FAR_ORDER = (6, 5, 7, 3, 4, 0, 2)
NEAR_ORDER = FAR_ORDER[::-1]
PLANE_ORDER = (10, 6, 14, 9, 11, 2, 8, 5, 7, 13, 15, 1, 3, 4, 12)


def kernel(
    hid,
    gain,
    wqkv,
    cache,
    lens,
    wout,
    out,
    raw_s,
    x_s,
    far_out,
    gain_s,
    wq_s,
    wkv_s,
    wo_s,
    cache_s,
    hrow_s,
    pq_s,
    rq_s,
    pkv_s,
    rkv_s,
    nkv_s,
    at_s,
    acc_s,
    po_s,
    ro_s,
    ps_s,
    fin_s,
    lsem,
    w_ss,
    w_rs,
    x_ss,
    x_rs,
    xp_ss,
    xp_rs,
    kv_ss,
    kv_rs,
    q_ss,
    q_rs,
    n_ss,
    n_rs,
    a_ss,
    a_rs,
    o_ss,
    o_rs,
    t_ss,
    t_rs,
    f_ss,
    f_rs,
    e_ss,
    e_rs,
):
    d = lax.axis_index("dp")
    t = lax.axis_index("tensor")
    k = t % 2
    c = t // 2
    cx = c // 4
    cy = c % 4
    half = c % 2
    row0 = pl.multiple_of(k * ROWS, ROWS)
    sibling = (d, c * 2 + (1 - k))
    sent = []

    def go(copy):
        copy.start()
        sent.append(copy)

    def block(g):
        return (d + REL[g]) % DP

    def at_block(g):
        return (block(g), t)

    def chip(o):
        px = (cx + o // 4) % 4
        py = (cy + o % 4) % 4
        return px * 4 + py

    def back(o):
        px = (cx + 4 - o // 4) % 4
        py = (cy + 4 - o % 4) % 4
        return px * 4 + py

    def rdma(src, dst, ss, rs, dev):
        return pltpu.make_async_remote_copy(
            src_ref=src, dst_ref=dst, send_sem=ss, recv_sem=rs, device_id=dev, device_id_type=MESH
        )

    def lanes(index):
        return pl.ds(pl.multiple_of(index * 128, 128), 128)

    def features(index):
        return pl.ds(pl.multiple_of(index * FEAT, FEAT), FEAT)

    l_gain = pltpu.make_async_copy(gain.at[:, features(d)], gain_s, lsem.at[1])
    l_x = pltpu.make_async_copy(hid.at[pl.ds(row0, ROWS), features(d)], raw_s.at[OWN], lsem.at[0])
    l_h = pltpu.make_async_copy(hid.at[pl.ds(row0, ROWS), :], hrow_s, lsem.at[2])
    l_wq = pltpu.make_async_copy(wqkv.at[:, pl.ds(0, QW)], wq_s.at[k], lsem.at[3])
    l_wkv = pltpu.make_async_copy(wqkv.at[:, lanes(4 + half)], wkv_s, lsem.at[4])
    l_cache = pltpu.make_async_copy(cache.at[pl.ds(row0, ROWS), 0], cache_s, lsem.at[5])
    l_wo = pltpu.make_async_copy(wout, wo_s.at[k], lsem.at[6])
    for copy in (l_gain, l_x, l_h, l_wkv, l_wq, l_cache, l_wo):
        copy.start()

    barrier = pltpu.get_barrier_semaphore()
    partners = [at_block(g) for g in FAR_ORDER]
    partners += [(d, chip(o) * 2 + k) for o in PLANE_ORDER]
    partners += [sibling]
    for dev in partners:
        pl.semaphore_signal(barrier, inc=1, device_id=dev, device_id_type=MESH)
    pl.semaphore_wait(barrier, len(partners))

    def x_copy(g):
        to = block(MIRROR[g])
        rows = pl.ds(row0, ROWS)
        if g < NEAR:
            return rdma(
                hid.at[rows, features(to)], raw_s.at[g], x_ss.at[g], x_rs.at[g], (to, t)
            )
        return rdma(
            hid.at[rows, lanes(to * (FEAT // 128) + c)],
            raw_s.at[g, :, lanes(c)],
            x_ss.at[g],
            x_rs.at[g],
            (to, t),
        )

    for g in FAR_ORDER:
        go(x_copy(g))
    go(rdma(wqkv.at[:, pl.ds(0, QW)], wq_s.at[k], w_ss.at[0], w_rs.at[0], sibling))

    l_h.wait()

    def square(i, total):
        cols = pl.ds(pl.multiple_of(i * 1024, 1024), 1024)
        part = hrow_s[:, cols].astype(F32)
        part = part * part
        for j in range(8):
            total = total + part[:, j * 128 : (j + 1) * 128]
        return total

    squares = lax.fori_loop(0, 16, square, jnp.zeros((ROWS, 128), F32))
    row_scale = lax.rsqrt(jnp.sum(squares, axis=1, keepdims=True) * (1.0 / (DP * FEAT)) + 1e-05)

    row_id = lax.broadcasted_iota(jnp.int32, (ROWS, HD), 0)
    lane_id = lax.broadcasted_iota(jnp.int32, (ROWS, HD), 1)
    length = jnp.zeros((ROWS, HD), jnp.int32)
    for b in range(ROWS):
        length = jnp.where(row_id == b, lens[k * ROWS + b], length)
    pair = jnp.where(lane_id < HD // 2, lane_id, lane_id - HD // 2).astype(F32)
    angle = length.astype(F32) * jnp.exp(pair * (-2.0 * math.log(ROPE_BASE) / HD))
    cosine = jnp.cos(angle)
    sine = jnp.sin(angle)
    sine = jnp.where(lane_id < HD // 2, -sine, sine)

    def rotate(v):
        return v * cosine + pltpu.roll(v, HD // 2, 1) * sine

    l_gain.wait()
    l_x.wait()

    def apply_gain(g):
        x_s[g] = (raw_s[g].astype(F32) * gain_s[...]).astype(BF16)

    apply_gain(OWN)

    for g in (3, 4, 5, 7, 6):
        x_copy(g).wait_recv()
    far = pl.ds(NEAR, DP - NEAR)
    tiles = raw_s[far, :, lanes(c)].astype(F32) * gain_s[:, lanes(c)].reshape(1, 1, 128)
    far_out[...] = tiles.astype(BF16)
    x_s[far, :, lanes(c)] = tiles.astype(BF16)

    def xp_copy(o, src):
        return rdma(
            far_out, x_s.at[far, :, lanes(src)], xp_ss.at[o], xp_rs.at[o], (d, chip(o) * 2 + k)
        )

    for o in PLANE_ORDER:
        go(xp_copy(o, c))

    for g in (0, 2):
        x_copy(g).wait_recv()
        apply_gain(g)

    def kv_copy(g):
        m = MIRROR[g]
        return rdma(pkv_s.at[g], rkv_s.at[m], kv_ss.at[g], kv_rs.at[m], at_block(g))

    def q_copy(s, g):
        m = MIRROR[g]
        return rdma(pq_s.at[s, g], rq_s.at[s, m], q_ss.at[s, g], q_rs.at[s, m], at_block(g))

    def project(lo, n, order):
        lhs = x_s[pl.ds(lo, n)].reshape(n * ROWS, FEAT)
        got = jnp.dot(lhs, wkv_s[...], preferred_element_type=F32)
        pkv_s[pl.ds(lo, n)] = got.astype(BF16).reshape(n, ROWS, HD)
        for g in order:
            go(kv_copy(g))
        for s in range(2):
            for j in range(2):
                cols = slice(j * 256, (j + 1) * 256)
                got = jnp.dot(lhs, wq_s[s, :, cols], preferred_element_type=F32)
                pq_s[s, pl.ds(lo, n), :, cols] = got.astype(BF16).reshape(n, ROWS, 256)
            for g in order:
                go(q_copy(s, g))

    go(rdma(wout, wo_s.at[k], w_ss.at[1], w_rs.at[1], sibling))
    l_wkv.wait()
    l_wq.wait()
    rdma(
        wqkv.at[:, pl.ds(0, QW)], wq_s.at[1 - k], w_ss.at[0], w_rs.at[0], sibling
    ).wait_recv()

    project(0, NEAR, (0, 2))

    for o in PLANE_ORDER[::-1]:
        xp_copy(o, back(o)).wait_recv()

    project(NEAR, DP - NEAR, (6, 5, 7, 3, 4))

    total = pkv_s[OWN].astype(F32)
    for g in NEAR_ORDER:
        kv_copy(MIRROR[g]).wait_recv()
        total = total + rkv_s[g].astype(F32)
    total = total * row_scale
    nkv_s[half] = jnp.where(half == 0, rotate(total), total).astype(BF16)
    beside = c + 1 - 2 * half

    def n_copy(which):
        return rdma(
            nkv_s.at[which], nkv_s.at[which], n_ss.at[0], n_rs.at[0], (d, beside * 2 + k)
        )

    go(n_copy(half))

    l_cache.wait()
    wide_row = lax.broadcasted_iota(jnp.int32, (4 * ROWS, HD), 0) % ROWS
    wide_lane = lax.broadcasted_iota(jnp.int32, (256, 4 * ROWS), 1) % ROWS
    position = lax.broadcasted_iota(jnp.int32, (4 * ROWS, 256), 1)
    limit = jnp.concatenate([length[:, :1]] * 4, axis=0)
    scale = 1.0 / HD**0.5

    def a_copy(s, g):
        m = MIRROR[g]
        return rdma(
            at_s.at[s, :, OWN], at_s.at[s, :, m], a_ss.at[s, g], a_rs.at[s, m], at_block(g)
        )

    for s in range(2):
        total = pq_s[s, OWN].astype(F32)
        for g in NEAR_ORDER:
            q_copy(s, MIRROR[g]).wait_recv()
            total = total + rq_s[s, g].astype(F32)
        total = total * row_scale

        queries = jnp.concatenate(
            [rotate(total[:, h * HD : (h + 1) * HD]) for h in range(4)], axis=0
        ).astype(BF16)
        turned = queries.astype(F32).T.astype(BF16)

        def score(i, scores):
            for j in range(4):
                b = i * 4 + j
                got = jnp.dot(cache_s[b, :, :HD], turned, preferred_element_type=F32)
                scores = jnp.where(wide_lane == b, got, scores)
            return scores

        scores = lax.fori_loop(0, 4, score, jnp.zeros((256, 4 * ROWS), F32))
        scores = jnp.where(position < limit, scores.T * scale, -jnp.inf)
        largest = jnp.max(scores, axis=1, keepdims=True)
        weights = jnp.exp(scores - largest)
        weight_sum = jnp.sum(weights, axis=1, keepdims=True)
        weights = weights.astype(BF16)

        def mix(i, mixed):
            for j in range(4):
                b = i * 4 + j
                got = jnp.dot(weights, cache_s[b, :, HD:], preferred_element_type=F32)
                mixed = jnp.where(wide_row == b, got, mixed)
            return mixed

        mixed = lax.fori_loop(0, 4, mix, jnp.zeros((4 * ROWS, HD), F32))
        if s == 0:
            n_copy(1 - half).wait_recv()
        new_key = jnp.concatenate([nkv_s[0].astype(F32)] * 4, axis=0)
        new_value = jnp.concatenate([nkv_s[1].astype(F32)] * 4, axis=0)
        own = jnp.sum(queries.astype(F32) * new_key, axis=1, keepdims=True) * scale
        top = jnp.maximum(largest, own)
        fade = jnp.exp(largest - top)
        own_weight = jnp.exp(own - top)
        attended = (mixed * fade + own_weight * new_value) / (weight_sum * fade + own_weight)
        at_s[s, :, OWN] = attended.astype(BF16).reshape(4, ROWS, HD)
        for g in FAR_ORDER:
            go(a_copy(s, g))

    l_wo.wait()
    rdma(wout, wo_s.at[1 - k], w_ss.at[1], w_rs.at[1], sibling).wait_recv()

    def heads(s):
        for g in NEAR_ORDER:
            a_copy(s, MIRROR[g]).wait_recv()
        return jnp.concatenate([at_s[s, h].reshape(DP * ROWS, HD) for h in range(4)], axis=1)

    def o_copy(to, slot):
        return rdma(po_s.at[to], ro_s.at[slot], o_ss.at[to], o_rs.at[slot], (d, to * 2 + k))

    lhs0 = heads(0)

    def first_half(i, carry):
        cols = pl.ds(pl.multiple_of(i * 256, 256), 256)
        acc_s[:, cols] = jnp.dot(lhs0, wo_s[0, :, cols], preferred_element_type=F32)
        return carry

    lax.fori_loop(0, 8, first_half, 0)
    lhs1 = heads(1)

    def second_half(i, carry):
        p = (cx + 2 + i // 2) % 4 * 2 + (cy // 2 + 1 + i) % 2
        cols = pl.ds(pl.multiple_of(p * 256, 256), 256)
        got = acc_s[:, cols] + jnp.dot(lhs1, wo_s[1, :, cols], preferred_element_type=F32)
        got = got.astype(BF16)
        for j in range(2):
            to = p * 2 + j
            po_s[to] = got[:, j * 128 : (j + 1) * 128].reshape(DP, ROWS, 128)

            @pl.when(to != c)
            def _():
                o_copy(to, c).start()

        return carry

    lax.fori_loop(0, 8, second_half, 0)
    for o in PLANE_ORDER:
        sent.append(o_copy(chip(o), c))

    total = po_s[c].astype(F32)
    for o in PLANE_ORDER[::-1]:
        src = back(o)
        o_copy(src, src).wait_recv()
        total = total + ro_s[src].astype(F32)
    ps_s[...] = (raw_s[:, :, lanes(c)].astype(F32) + total).astype(BF16)

    def t_copy(g):
        return rdma(ps_s.at[g], fin_s.at[d], t_ss.at[g], t_rs.at[MIRROR[g]], at_block(g))

    for g in FAR_ORDER:
        go(t_copy(g))
    fin_s[d] = ps_s[OWN]

    def f_copy(q, o, src, which):
        return rdma(
            fin_s.at[which],
            out.at[k, which, :, lanes(src)],
            f_ss.at[q, o],
            f_rs.at[q, o],
            (d, chip(o) * 2 + k),
        )

    def f_all(q, o, src):
        return f_copy(q, o, src, pl.ds(0, len(PARTS[q])))

    earlier = list(sent)
    sent.clear()
    for q, part in enumerate(PARTS):
        for g in part:
            if g != OWN:
                rdma(
                    ps_s.at[g], fin_s.at[block(g)], t_ss.at[g], t_rs.at[g], at_block(g)
                ).wait_recv()
        for o in PLANE_ORDER:
            for g in part:
                f_copy(q, o, c, block(g)).start()
            sent.append(f_all(q, o, c))

    def e_copy(o, src, half_of):
        view = out.at[half_of, :, :, lanes(src)]
        return rdma(view, view, e_ss.at[o], e_rs.at[o], sibling)

    out[k, :, :, lanes(c)] = fin_s[...]
    go(e_copy(0, c, k))
    for copy in earlier:
        copy.wait_send()
    for o in PLANE_ORDER[::-1]:
        for q in range(len(PARTS)):
            f_all(q, o, back(o)).wait_recv()
        go(e_copy(o, back(o), k))

    e_copy(0, c, 1 - k).wait_recv()
    for o in PLANE_ORDER[::-1]:
        e_copy(o, back(o), 1 - k).wait_recv()

    for copy in sent:
        copy.wait_send()


def body(hidden, gain, w_qkv, cache, lengths, w_out):
    any_space = pl.BlockSpec(memory_space=pl.ANY)
    vmem = pltpu.VMEM
    dma = pltpu.SemaphoreType.DMA
    scratch = [
        vmem((DP, ROWS, FEAT), BF16),
        vmem((DP, ROWS, FEAT), BF16),
        vmem((DP - NEAR, ROWS, 128), BF16),
        vmem((1, FEAT), F32),
        vmem((2, FEAT, QW), BF16),
        vmem((FEAT, HD), BF16),
        vmem((2, QW, FEAT), BF16),
        vmem((ROWS, 256, 256), BF16),
        vmem((ROWS, DP * FEAT), BF16),
        vmem((2, DP, ROWS, QW), BF16),
        vmem((2, DP, ROWS, QW), BF16),
        vmem((DP, ROWS, HD), BF16),
        vmem((DP, ROWS, HD), BF16),
        vmem((2, ROWS, HD), BF16),
        vmem((2, 4, DP, ROWS, HD), BF16),
        vmem((DP * ROWS, FEAT), F32),
        vmem((CHIPS, DP, ROWS, 128), BF16),
        vmem((CHIPS, DP, ROWS, 128), BF16),
        vmem((DP, ROWS, 128), BF16),
        vmem((DP, ROWS, 128), BF16),
        dma((7,)),
        dma((2,)),
        dma((2,)),
        dma((DP,)),
        dma((DP,)),
        dma((CHIPS,)),
        dma((CHIPS,)),
        dma((DP,)),
        dma((DP,)),
        dma((2, DP)),
        dma((2, DP)),
        dma((1,)),
        dma((1,)),
        dma((2, DP)),
        dma((2, DP)),
        dma((CHIPS,)),
        dma((CHIPS,)),
        dma((DP,)),
        dma((DP,)),
        dma((len(PARTS), CHIPS)),
        dma((len(PARTS), CHIPS)),
        dma((CHIPS,)),
        dma((CHIPS,)),
    ]
    halves = pl.pallas_call(
        kernel,
        out_shape=vmem((2, DP, ROWS, FEAT), BF16),
        in_specs=[
            any_space,
            any_space,
            any_space,
            any_space,
            pl.BlockSpec(memory_space=pltpu.SMEM),
            any_space,
        ],
        out_specs=pl.BlockSpec(memory_space=vmem),
        scratch_shapes=scratch,
        compiler_params=pltpu.CompilerParams(
            collective_id=0, has_side_effects=True, vmem_limit_bytes=60 * 1024 * 1024
        ),
    )(hidden, gain.reshape(1, -1), w_qkv, cache, lengths, w_out)
    tiles = halves.reshape(2, DP, 2, 8, FEAT).transpose(0, 2, 3, 1, 4)
    return tiles.reshape(hidden.shape)


def solution(mesh):
    return jax.shard_map(
        body,
        mesh=mesh,
        in_specs=(
            P("dp", None),
            P(),
            P("dp", "tensor"),
            P("dp", "tensor", None, None),
            P("dp"),
            P("tensor", "dp"),
        ),
        out_specs=P("dp", None),
        check_vma=False,
    )
```
